128 devices in a mesh: row: 8 (over y, z_hi), col: 16 (over z_lo, x, core).
Axes of the slice: x: 4, y: 4, z: 4 (z_hi: 2, z_lo: 2; z = z_hi * 2 + z_lo), core: 2. Of those that a mesh axis runs over, the one named last changes fastest.
Arguments:
- hamil: bfloat16 [4096, 4096], P('row', 'col'), as said below
- guess: bfloat16 [4096, 4096], P('row', 'col'), as said below
- pattern: int32 [64, 64], P('row', 'col'), may hold values from 0 to 1, as said below
- filters: int32 [2, 64, 64], P(None, 'row', 'col'), may hold values from 0 to 1, as said below
- deriv: bfloat16 [3, 4096, 4096], P(None, ('row', 'col')), may hold values from -6 to 6
- atom_of_row: int32 [4096], P(('row', 'col')), may hold values from 0 to 3, as said below
Outputs:
- owned_energy: bfloat16 [4096, 4096], P(('row', 'col'))
- forces: float32 [3, 512], P(None, ('row', 'col'))
The draws below stay inside these ranges and needn't reach their ends.
Inputs may be any that keep to these rules, and one draw needn't show every extreme that they name: `atom_of_row`: within each aligned block of 32 rows (d * 32 to (d + 1) * 32 - 1) the ids never fall, begin at 0, end at 3, and every id from 0 to 3 has one row or more. Symmetric: hamil equals its transpose. Symmetric: guess equals its transpose. Symmetric 0/1 block pattern. `filters`: each step's 0/1 mask is symmetric.
All inputs are finite; a program needn't handle non-finite values.
Results may differ from the reference program's by a relative error of at most 0.04.
Values may be sent and summed in bfloat16 or wider, within the bound.
A program may use at most 64 MiB of HBM per device.

```python
import jax
import jax.numpy as jnp
from jax import lax

BS = 64
STEPS = 2
ATOM_DEV = 4
NB = 64
N = 4096
OWN = 32
ATOMS = 512


def symmetric_normal(key, spread):
    values = jnp.clip(jax.random.normal(key, (N, N), jnp.float32), -6.0, 6.0) * spread
    return ((values + values.T) * 0.7071067811865476).astype(jnp.bfloat16)


def draw_hamil(key, part):
    key = jax.random.fold_in(key, 3)
    return symmetric_normal(key, (1.0 * N) ** (-0.5))


def draw_guess(key, part):
    key = jax.random.fold_in(key, 5)
    return symmetric_normal(key, (8.0 * N) ** (-0.5))


def draw_pattern(key, part):
    key = jax.random.fold_in(key, 11)
    picks = (jax.random.randint(key, (NB, NB), 0, 10) < 3).astype(jnp.int32)
    return jnp.maximum(picks, picks.T).astype(jnp.int32)


def draw_filters(key, part):
    key = jax.random.fold_in(key, 13)
    picks = (jax.random.randint(key, (STEPS, NB, NB), 0, 2) < 1).astype(jnp.int32)
    return jnp.maximum(picks, jnp.transpose(picks, (0, 2, 1))).astype(jnp.int32)


def draw_atom_of_row(key, part):
    key = jax.random.fold_in(key, 7)
    owners = N // OWN
    scores = jax.random.randint(key, (owners, OWN - 1), 0, 1 << 20) * OWN + jnp.arange(OWN - 1, dtype=jnp.int32)[None, :]
    order = jnp.argsort(scores, axis=1, stable=True)
    cut_points = order[:, :ATOM_DEV - 1] + 1
    positions = jnp.arange(OWN, dtype=jnp.int32)
    labels = jnp.sum((positions[None, :, None] >= cut_points[:, None, :]).astype(jnp.int32), axis=2)
    return labels.reshape(N).astype(jnp.int32)


def levels(key, dims, split, smallest, largest):
    factor_of = 1.0
    for axis_at, parts in split:
        steps = jax.random.uniform(jax.random.fold_in(jax.random.fold_in(key, 6), axis_at), (parts,), jnp.float32, smallest / len(split), largest / len(split))
        factor_of = factor_of * jnp.repeat(jnp.exp(steps), dims[axis_at] // parts).reshape((-1,) + (1,) * (len(dims) - 1 - axis_at))
    return factor_of


def bell_draw(rng, shape, scale, limit, split=(), kind=jnp.bfloat16):
    array = scale * jax.random.normal(rng, shape, jnp.float32)
    if split:
        array = array * levels(rng, shape, split, -0.22, 0.18)
    return jnp.clip(array, -limit, limit).astype(kind)


def setup_inputs(seed: int = 0) -> dict:
    keys = jax.random.split(jax.random.key(seed), 7)
    hamil = draw_hamil(jax.random.fold_in(keys[6], 71), 0)
    guess = draw_guess(jax.random.fold_in(keys[6], 71), 0)
    pattern = draw_pattern(jax.random.fold_in(keys[6], 71), 0)
    filters = draw_filters(jax.random.fold_in(keys[6], 71), 0)
    deriv = bell_draw(keys[4], (3, N, N), 1.0, 6.0, ((1, 128),))
    atom_of_row = draw_atom_of_row(jax.random.fold_in(keys[6], 71), 0)
    return dict(hamil=hamil, guess=guess, pattern=pattern, filters=filters, deriv=deriv, atom_of_row=atom_of_row)


def expand(block_mask):
    return jnp.repeat(jnp.repeat(block_mask.astype(jnp.float32), BS, 0), BS, 1)


def reference(hamil, guess, pattern, filters, deriv, atom_of_row):
    kept_mask = expand(pattern)
    density = (0.5 * jnp.eye(N, dtype=jnp.float32) + guess.astype(jnp.float32)) * kept_mask
    for purify_step in range(STEPS):
        dens_bf = density.astype(jnp.bfloat16)
        square = jnp.dot(dens_bf, dens_bf, preferred_element_type=jnp.float32)
        square_bf = square.astype(jnp.bfloat16)
        cube_term = jnp.dot(square_bf, dens_bf, preferred_element_type=jnp.float32)
        density = expand(filters[purify_step]) * (3.0 * square - 2.0 * cube_term)
    final_bf = density.astype(jnp.bfloat16)
    ham_bf = jnp.where(kept_mask > 0, hamil, jnp.zeros_like(hamil))
    ham_dens = jnp.dot(ham_bf, final_bf, preferred_element_type=jnp.float32).astype(jnp.bfloat16)
    owned_energy = jnp.dot(final_bf, ham_dens, preferred_element_type=jnp.float32).astype(jnp.bfloat16)
    energy_wide = owned_energy.astype(jnp.float32)
    per_row = jnp.stack([jnp.sum(deriv[axis_num].astype(jnp.float32) * energy_wide, axis=1) for axis_num in range(3)])
    owners = N // OWN
    onehot = (atom_of_row[:, None] == jnp.arange(ATOM_DEV, dtype=jnp.int32)[None, :]).astype(jnp.float32)
    forces = jnp.einsum("xdo,doa->xda", per_row.reshape(3, owners, OWN), onehot.reshape(owners, OWN, ATOM_DEV), precision=lax.Precision.HIGHEST)
    return owned_energy, forces.reshape(3, ATOMS)
```

```python
import functools

import jax
import jax.numpy as jnp
from jax import lax
from jax.experimental import pallas as pl
from jax.experimental.pallas import tpu as pltpu
from jax.sharding import PartitionSpec as P

MESH = pl.DeviceIdType.MESH
BS = 64
ATOM_DEV = 4
ROWS, COLS, OWN, N = 512, 256, 32, 4096
BF, F32 = jnp.bfloat16, jnp.float32


class Place:
    def __init__(self):
        self.r, self.c = lax.axis_index("row"), lax.axis_index("col")
        self.y, self.zh = self.r // 2, self.r % 2
        self.zl, self.x, self.k = self.c // 8, (self.c // 2) % 4, self.c % 2

    def col(self, dz, dx, dk=0):
        return ((self.zl + dz) % 2) * 8 + ((self.x + dx) % 4) * 2 + (self.k + dk) % 2

    def row(self, dz, dy):
        return ((self.y + dy) % 4) * 2 + (self.zh + dz) % 2

    def along(self, dz, dx, dk=0):
        return (self.r, self.col(dz, dx, dk))

    def across(self, dz, dy):
        return (self.row(dz, dy), self.c)


class Copies:
    def __init__(self, send_sems, recv_sems):
        self.send_sems, self.recv_sems = send_sems, recv_sems
        self.sent, self.n_send, self.n_recv = [], 0, 0

    def take(self, count):
        first = self.n_recv
        self.n_recv += count
        return first

    def make(self, src, dst, recv, device, send):
        return pltpu.make_async_remote_copy(
            src_ref=src,
            dst_ref=dst,
            send_sem=self.send_sems.at[send],
            recv_sem=self.recv_sems.at[recv],
            device_id=device,
            device_id_type=MESH,
        )

    def send(self, src, dst, recv, device):
        copy = self.make(src, dst, recv, device, self.n_send)
        self.n_send += 1
        copy.start()
        self.sent.append(copy)
        return copy

    def arrive(self, ref, recv, device):
        self.make(ref, ref, recv, device, 0).wait_recv()

    def drain(self, copies=None):
        for copy in list(self.sent if copies is None else copies):
            copy.wait_send()
            self.sent = [other for other in self.sent if other is not copy]


def block_cols(buf, c):
    return buf.at[:, pl.ds(pl.multiple_of(c * COLS, COLS), COLS)]


def block_rows(buf, r):
    return buf.at[pl.ds(pl.multiple_of(r * ROWS, ROWS), ROWS)]


class Gather:
    def __init__(self, cp, me, buf, axis):
        self.cp, self.me, self.buf, self.axis = cp, me, buf, axis
        self.sent = []
        self.recv = cp.take(8)
        self.side = cp.take(8) if axis == "col" else None

    def slot(self, dz, d, dk=0):
        if self.axis == "col":
            return block_cols(self.buf, self.me.col(dz, d, dk))
        return block_rows(self.buf, self.me.row(dz, d))

    def peer(self, dz, d):
        return self.me.along(dz, d) if self.axis == "col" else self.me.across(dz, d)

    def push(self, dz):
        block = self.slot(dz, 0)
        for d in (1, 3, 2):
            self.sent.append(self.cp.send(block, block, self.recv + dz * 4 + d, self.peer(0, d)))

    def share(self, dz, d):
        if self.axis == "col":
            block = self.slot(dz, -d)
            self.sent.append(self.cp.send(block, block, self.side + dz * 4 + d, self.me.along(0, 0, 1)))

    def start(self):
        block = self.slot(0, 0)
        self.sent.append(self.cp.send(block, block, self.recv + 4, self.peer(1, 0)))
        self.push(0)
        self.share(0, 0)

    def arrive(self, dz, d):
        self.cp.arrive(self.slot(dz, -d), self.recv + dz * 4 + d, self.peer(1, 0))
        self.share(dz, d)

    def forward(self):
        self.arrive(1, 0)
        self.push(1)

    def arrive_side(self, dz, d):
        self.cp.arrive(self.slot(dz, -d, 1), self.side + dz * 4 + d, self.peer(1, 0))


ORDER = [(0, 1), (0, 3), (0, 2), (1, 1), (1, 3), (1, 2)]


def gather_all(gathers):
    for g in gathers:
        g.forward()
    for dz, d in ORDER:
        for g in gathers:
            g.arrive(dz, d)


def dot(a, b):
    return jnp.dot(a, b, preferred_element_type=F32)


def mask_rows(read):
    lane = lax.broadcasted_iota(jnp.int32, (1, COLS), 1) // BS
    out = []
    for i in range(ROWS // BS):
        row = jnp.zeros((1, COLS), F32)
        for j in range(COLS // BS):
            row = jnp.where(lane == j, read(i, j).astype(F32), row)
        out.append(row)
    return out


def kernel(
    hamil, guess, pattern, filters, deriv, atoms,
    energy_out, forces_out,
    rowp, colp, srow, hcol, square, etile, eall, send_sems, recv_sems,
):
    me = Place()
    cp = Copies(send_sems, recv_sems)
    peers = [me.along(dz, dx, dk) for dz in range(2) for dx in range(4) for dk in range(2)][1:]
    peers += [me.across(0, 1), me.across(0, 2), me.across(0, 3), me.across(1, 0)]
    barrier = pltpu.get_barrier_semaphore()
    for peer in peers:
        pl.semaphore_signal(barrier, inc=1, device_id=peer, device_id_type=MESH)

    kept = mask_rows(lambda i, j: pattern[i, j])
    own_row, own_col = block_cols(rowp, me.c), block_rows(colp.at[0], me.r)
    own_ham = block_rows(hcol, me.r)
    for i in range(ROWS // BS):
        part = slice(i * BS, (i + 1) * BS)
        here = me.r * ROWS + i * BS + lax.broadcasted_iota(jnp.int32, (BS, COLS), 0)
        there = me.c * COLS + lax.broadcasted_iota(jnp.int32, (BS, COLS), 1)
        half = jnp.where(here == there, 0.5, 0.0).astype(F32)
        dens = ((half + guess[part].astype(F32)) * kept[i]).astype(BF)
        own_row[part] = dens
        own_col[part] = dens
        own_ham[part] = jnp.where(kept[i] > 0, hamil[part].astype(F32), 0.0).astype(BF)
    pl.semaphore_wait(barrier, len(peers))

    ham = None
    for step in range(3):
        panel = colp.at[step % 2]
        rows, cols = Gather(cp, me, rowp, "col"), Gather(cp, me, panel, "row")
        rows.start()
        cols.start()
        gather_all([rows, cols])
        for dz, d in [(0, 0), (1, 0)] + ORDER:
            rows.arrive_side(dz, d)
        if step == 2:
            for dz, d in ORDER:
                ham.arrive(dz, d)
        cp.drain()
        first = dot(rowp[...], hcol[...] if step == 2 else panel[...])
        own = block_cols(srow, me.c)
        own[...] = first.astype(BF)
        inner = Gather(cp, me, srow, "col")
        inner.start()
        if step == 0:
            ham = Gather(cp, me, hcol, "row")
            ham.start()
        if step < 2:
            square[...] = first
        inner.forward()
        if step == 0:
            ham.forward()
        total = None
        for dk in range(2):
            for dz, d in [(0, 0), (1, 0)] + ORDER:
                if dk == 1:
                    inner.arrive_side(dz, d)
                elif (dz, d) in ORDER:
                    inner.arrive(dz, d)
                at = pl.ds(pl.multiple_of(me.col(dz, -d, dk) * COLS, COLS), COLS)
                term = dot(srow[:, at], panel[at])
                total = term if total is None else total + term
        cp.drain(inner.sent)
        if step < 2:
            keep = mask_rows(lambda i, j: filters[step, i, j])
            after = block_rows(colp.at[(step + 1) % 2], me.r)
            for i in range(ROWS // BS):
                part = slice(i * BS, (i + 1) * BS)
                dens = (keep[i] * (3.0 * square[part] - 2.0 * total[part])).astype(BF)
                own_row[part] = dens
                after[part] = dens
        else:
            etile[...] = total.astype(BF)

    base = cp.take(16)
    mine = pl.ds(pl.multiple_of(me.c * COLS, COLS), COLS)
    rels = [(dz, dx, dk) for dx in (2, 1, 3, 0) for dz in (1, 0) for dk in range(2)]
    rels.remove((0, 0, 0))
    for dz, dx, dk in rels:
        target = me.col(dz, dx, dk)
        src = etile.at[pl.ds(pl.multiple_of(target * OWN, OWN), OWN)]
        cp.send(src, eall.at[:, mine], base + dz * 8 + dx * 2 + dk, (me.r, target))
    eall[:, mine] = etile[pl.ds(pl.multiple_of(me.c * OWN, OWN), OWN)]
    for dz, dx, dk in rels:
        cp.arrive(block_cols(eall, me.col(dz, -dx, dk)), base + dz * 8 + dx * 2 + dk, me.along(1, 0))
    energy = eall[...]
    energy_out[...] = energy
    wide = energy.astype(F32)
    line = lax.broadcasted_iota(jnp.int32, (3, ATOM_DEV), 0)
    lane = lax.broadcasted_iota(jnp.int32, (3, ATOM_DEV), 1)
    forces = jnp.zeros((3, ATOM_DEV), F32)
    for axis in range(3):
        per_row = jnp.sum(deriv[axis].astype(F32) * wide, axis=1, keepdims=True)
        for atom in range(ATOM_DEV):
            force = jnp.sum(jnp.where(atoms[...] == atom, per_row, 0.0))
            forces = jnp.where((line == axis) & (lane == atom), force, forces)
    forces_out[...] = forces
    cp.drain()


def body(hamil, guess, pattern, filters, deriv, atom_of_row):
    vmem, smem = pl.BlockSpec(memory_space=pltpu.VMEM), pl.BlockSpec(memory_space=pltpu.SMEM)
    return pl.pallas_call(
        kernel,
        out_shape=(
            jax.ShapeDtypeStruct((OWN, N), BF),
            jax.ShapeDtypeStruct((3, ATOM_DEV), F32),
        ),
        in_specs=[vmem, vmem, smem, smem, vmem, vmem],
        out_specs=(vmem, vmem),
        scratch_shapes=[
            pltpu.VMEM((ROWS, N), BF),
            pltpu.VMEM((2, N, COLS), BF),
            pltpu.VMEM((ROWS, N), BF),
            pltpu.VMEM((N, COLS), BF),
            pltpu.VMEM((ROWS, COLS), F32),
            pltpu.VMEM((ROWS, COLS), BF),
            pltpu.VMEM((OWN, N), BF),
            pltpu.SemaphoreType.DMA((160,)),
            pltpu.SemaphoreType.DMA((160,)),
        ],
        compiler_params=pltpu.CompilerParams(
            collective_id=0, has_side_effects=True, vmem_limit_bytes=48 * 1024 * 1024
        ),
    )(hamil, guess, pattern, filters, deriv, atom_of_row.reshape(OWN, 1))


def solution(mesh):
    return jax.shard_map(
        body,
        mesh=mesh,
        in_specs=(
            P("row", "col"),
            P("row", "col"),
            P("row", "col"),
            P(None, "row", "col"),
            P(None, ("row", "col"), None),
            P(("row", "col")),
        ),
        out_specs=(P(("row", "col"), None), P(None, ("row", "col"))),
        check_vma=False,
    )
```

```python
import functools

import jax
import jax.numpy as jnp
from jax import lax
from jax.experimental import pallas as pl
from jax.experimental.pallas import tpu as pltpu
from jax.sharding import PartitionSpec as P

MESH = pl.DeviceIdType.MESH
BS = 64
ATOM_DEV = 4
ROWS, COLS, OWN, N = 512, 256, 32, 4096
BF, F32 = jnp.bfloat16, jnp.float32
CHUNKS = 2
CHUNK = ROWS // CHUNKS
ORDER = [h + i for h in range(CHUNKS // 2) for i in (0, CHUNKS // 2)]


class Place:
    def __init__(self):
        self.r, self.c = lax.axis_index("row"), lax.axis_index("col")
        self.y, self.zh = self.r // 2, self.r % 2
        self.zl, self.x, self.k = self.c // 8, (self.c // 2) % 4, self.c % 2

    def col(self, dz, dx, dk=0):
        return ((self.zl + dz) % 2) * 8 + ((self.x + dx) % 4) * 2 + (self.k + dk) % 2

    def row(self, dz, dy):
        return ((self.y + dy) % 4) * 2 + (self.zh + dz) % 2

    def along(self, dz, dx, dk=0):
        return (self.r, self.col(dz, dx, dk))

    def across(self, dz, dy):
        return (self.row(dz, dy), self.c)


class Copies:
    def __init__(self, send_sems, recv_sems):
        self.send_sems, self.recv_sems = send_sems, recv_sems

    def make(self, src, dst, send, recv, device):
        return pltpu.make_async_remote_copy(
            src_ref=src,
            dst_ref=dst,
            send_sem=self.send_sems.at[send],
            recv_sem=self.recv_sems.at[recv],
            device_id=device,
            device_id_type=MESH,
        )

    def send(self, src, dst, send, recv, device):
        self.make(src, dst, send, recv, device).start()

    def arrive(self, ref, recv, device):
        self.make(ref, ref, 0, recv, device).wait_recv()

    def sent(self, ref, send, device):
        self.make(ref, ref, send, 0, device).wait_send()


def tile_cols(buf, c, lo=0, size=ROWS):
    return buf.at[lo : lo + size, pl.ds(pl.multiple_of(c * COLS, COLS), COLS)]


def tile_rows(buf, r, lo=0, size=ROWS):
    return buf.at[pl.ds(pl.multiple_of(r * ROWS + lo, size), size)]


class Gather:
    RECV = 2 * (CHUNKS + 2) + CHUNKS

    def __init__(self, cp, me, buf, axis, send, recv):
        self.cp, self.me, self.buf, self.axis = cp, me, buf, axis
        self.send, self.recv = send, recv

    def ref(self, dz, d, lo=0, size=ROWS, dk=0):
        if self.axis == "col":
            return tile_cols(self.buf, self.me.col(dz, d, dk), lo, size)
        return tile_rows(self.buf, self.me.row(dz, d), lo, size)

    def chunk(self, dz, d, h):
        return self.ref(dz, d, h * CHUNK, CHUNK)

    def peer(self, dz, d):
        return self.me.along(dz, d) if self.axis == "col" else self.me.across(dz, d)

    def put(self, ref, recv, device):
        self.cp.send(ref, ref, self.send, self.recv + recv, device)

    def got(self, ref, recv):
        self.cp.arrive(ref, self.recv + recv, self.peer(1, 0))

    def at(self, dz, d, h):
        passed = (d == 1 and h < CHUNKS // 2) or (d == 3 and h >= CHUNKS // 2)
        return CHUNKS + dz * (CHUNKS + 2) + (h if passed else CHUNKS if d != 2 else CHUNKS + 1)

    def push(self, dz, d, h):
        self.put(self.chunk(dz, 0, h), self.at(dz, d, h), self.peer(0, d))

    def pass_on(self, dz):
        for h in ORDER:
            d = 1 if h < CHUNKS // 2 else 3
            self.got(self.chunk(dz, -d, h), self.at(dz, d, h))
            self.put(self.chunk(dz, -d, h), self.at(dz, 2, h), self.peer(0, d))

    def share(self, dz, d):
        if self.axis == "col":
            self.put(self.ref(dz, -d), Gather.RECV + dz * 4 + d, self.me.along(0, 0, 1))

    def start(self):
        for h in ORDER:
            self.put(self.chunk(0, 0, h), h, self.peer(1, 0))
        for h in ORDER:
            self.push(0, 1 if h < CHUNKS // 2 else 3, h)
        for h in ORDER:
            self.push(0, 3 if h < CHUNKS // 2 else 1, h)
        self.share(0, 0)

    def push_partner(self):
        for h in ORDER:
            self.got(self.chunk(1, 0, h), h)
            self.push(1, 1 if h < CHUNKS // 2 else 3, h)
        for h in ORDER:
            self.push(1, 3 if h < CHUNKS // 2 else 1, h)
        self.share(1, 0)

    def near(self, dz):
        self.got(self.ref(dz, 0), self.at(dz, 1, CHUNKS - 1))
        self.share(dz, 1)
        self.share(dz, 3)

    def far(self, dz):
        self.got(self.ref(dz, 2), self.at(dz, 2, 0))
        self.share(dz, 2)

    def shared(self, dz, d):
        self.got(self.ref(dz, -d, dk=1), Gather.RECV + dz * 4 + d)

    def drain(self):
        count = 7 + (8 if self.axis == "col" else 0)
        if self.axis == "col":
            whole = self.buf.at[:, : count * COLS]
        else:
            whole = self.buf.at[: count * ROWS]
        self.cp.sent(whole, self.send, self.peer(1, 0))


PARTS = [
    lambda g: g.start(),
    lambda g: g.pass_on(0),
    lambda g: g.push_partner(),
    lambda g: g.near(0),
    lambda g: g.pass_on(1),
    lambda g: g.far(0),
    lambda g: g.near(1),
    lambda g: g.far(1),
]
TILES = [(dz, d) for dz in range(2) for d in (0, 1, 3, 2)]


def dot(a, b):
    return jnp.dot(a, b, preferred_element_type=F32)


def mask_rows(blocks):
    lane = lax.broadcasted_iota(jnp.int32, (1, COLS), 1) // BS
    blocks = blocks.astype(F32)
    out = []
    for i in range(ROWS // BS):
        row = jnp.zeros((1, COLS), F32)
        for j in range(COLS // BS):
            row = jnp.where(lane == j, blocks[i : i + 1, j : j + 1], row)
        out.append(row)
    return out


def kernel(
    hamil_hbm, guess_hbm, pattern_hbm, filters_hbm, deriv_hbm, atoms_hbm,
    energy_out, forces_out,
    hamil, guess, pattern, filters, deriv, atoms,
    rowp, colp, srow, hcol, square, etile, eall, load_sems, send_sems, recv_sems,
):
    me = Place()
    cp = Copies(send_sems, recv_sems)
    peers = [me.along(dz, dx, dk) for dz in range(2) for dx in range(4) for dk in range(2)][1:]
    peers += [me.across(0, 1), me.across(0, 2), me.across(0, 3), me.across(1, 0)]
    barrier = pltpu.get_barrier_semaphore()
    for peer in peers:
        pl.semaphore_signal(barrier, inc=1, device_id=peer, device_id_type=MESH)

    pairs = [(pattern_hbm, pattern), (guess_hbm, guess), (hamil_hbm, hamil)]
    pairs += [(filters_hbm, filters), (deriv_hbm, deriv), (atoms_hbm, atoms)]
    loads = [pltpu.make_async_copy(a, b, load_sems.at[i]) for i, (a, b) in enumerate(pairs)]
    for load in loads:
        load.start()
    for load in loads[:3]:
        load.wait()

    kept = mask_rows(pattern[...])
    own_row = tile_cols(rowp, me.c)
    own_col = [tile_rows(colp.at[i], me.r) for i in range(2)]
    own_ham = tile_rows(hcol, me.r)
    for i in range(ROWS // BS):
        part = slice(i * BS, (i + 1) * BS)
        here = me.r * ROWS + i * BS + lax.broadcasted_iota(jnp.int32, (BS, COLS), 0)
        there = me.c * COLS + lax.broadcasted_iota(jnp.int32, (BS, COLS), 1)
        half = jnp.where(here == there, 0.5, 0.0).astype(F32)
        dens = ((half + guess[part].astype(F32)) * kept[i]).astype(BF)
        own_row[part] = dens
        own_col[0][part] = dens
        own_ham[part] = jnp.where(kept[i] > 0, hamil[part].astype(F32), 0.0).astype(BF)
    pl.semaphore_wait(barrier, len(peers))

    step_sems = Gather.RECV + 8
    for step in range(3):
        panel = colp.at[step % 2]
        rows = Gather(cp, me, rowp, "col", 0, 0)
        inner = Gather(cp, me, srow, "col", 1, step_sems)
        cols = Gather(cp, me, panel, "row", 2 + step % 2, 2 * step_sems + step % 2 * Gather.RECV)
        ham = Gather(cp, me, hcol, "row", 4, 2 * step_sems + 2 * Gather.RECV)
        for part in PARTS:
            part(rows)
            part(cols)
        for dz, d in TILES:
            rows.shared(dz, d)
        rows.drain()
        cols.drain()
        first = dot(rowp[...], hcol[...] if step == 2 else panel[...])
        tile_cols(srow, me.c)[...] = first.astype(BF)

        total = None

        def add(dk, *tiles):
            nonlocal total
            for dz, d in tiles:
                if dk:
                    inner.shared(dz, d)
                at = pl.ds(pl.multiple_of(me.col(dz, -d, dk) * COLS, COLS), COLS)
                term = dot(srow[:, at], panel[at])
                total = term if total is None else total + term

        for i, part in enumerate(PARTS):
            part(inner)
            if step == 0:
                part(ham)
            if i == 0:
                if step < 2:
                    square[...] = first
                add(0, (0, 0))
            if i == 2:
                add(1, (0, 0))
            if i == 4:
                add(0, (0, 1), (0, 3), (1, 0))
            if i == 5:
                add(1, (0, 1), (0, 3), (1, 0))
            if i == 6:
                add(0, (0, 2), (1, 1), (1, 3))
                add(1, (0, 2))
            if i == 7:
                add(1, (1, 1), (1, 3))
                add(0, (1, 2))
                add(1, (1, 2))
        inner.drain()
        if step == 0:
            ham.drain()
        if step < 2:
            if step == 0:
                loads[3].wait()
            keep = mask_rows(filters[step])
            for i in range(ROWS // BS):
                part = slice(i * BS, (i + 1) * BS)
                dens = (keep[i] * (3.0 * square[part] - 2.0 * total[part])).astype(BF)
                own_row[part] = dens
                own_col[(step + 1) % 2][part] = dens
        else:
            etile[...] = total.astype(BF)

    out_sem = 2 * step_sems + 3 * Gather.RECV
    rels = [(dz, dx, dk) for dx in (2, 1, 3, 0) for dz in (1, 0) for dk in range(2)]
    rels.remove((0, 0, 0))
    for dz, dx, dk in rels:
        target = me.col(dz, dx, dk)
        src = etile.at[pl.ds(pl.multiple_of(target * OWN, OWN), OWN)]
        cp.send(src, tile_cols(eall, me.c, 0, OWN), 5, out_sem, (me.r, target))
    tile_cols(eall, me.c, 0, OWN)[...] = etile[pl.ds(pl.multiple_of(me.c * OWN, OWN), OWN)]
    others = eall.at[:, : len(rels) * COLS]
    cp.arrive(others, out_sem, me.along(1, 0))
    cp.sent(others, 5, me.along(1, 0))
    loads[4].wait()
    loads[5].wait()
    energy = eall[...]
    energy_out[...] = energy
    wide = energy.astype(F32)
    line = lax.broadcasted_iota(jnp.int32, (3, ATOM_DEV), 0)
    lane = lax.broadcasted_iota(jnp.int32, (3, ATOM_DEV), 1)
    forces = jnp.zeros((3, ATOM_DEV), F32)
    for axis in range(3):
        per_row = jnp.sum(deriv[axis].astype(F32) * wide, axis=1, keepdims=True)
        for atom in range(ATOM_DEV):
            force = jnp.sum(jnp.where(atoms[...] == atom, per_row, 0.0))
            forces = jnp.where((line == axis) & (lane == atom), force, forces)
    forces_out[...] = forces


def body(hamil, guess, pattern, filters, deriv, atom_of_row):
    args = (hamil, guess, pattern, filters, deriv, atom_of_row.reshape(OWN, 1))
    vmem = pl.BlockSpec(memory_space=pltpu.VMEM)
    return pl.pallas_call(
        kernel,
        out_shape=(
            jax.ShapeDtypeStruct((OWN, N), BF),
            jax.ShapeDtypeStruct((3, ATOM_DEV), F32),
        ),
        in_specs=[pl.BlockSpec(memory_space=pl.ANY)] * 6,
        out_specs=(vmem, vmem),
        scratch_shapes=[pltpu.VMEM(arg.shape, arg.dtype) for arg in args]
        + [
            pltpu.VMEM((ROWS, N), BF),
            pltpu.VMEM((2, N, COLS), BF),
            pltpu.VMEM((ROWS, N), BF),
            pltpu.VMEM((N, COLS), BF),
            pltpu.VMEM((ROWS, COLS), F32),
            pltpu.VMEM((ROWS, COLS), BF),
            pltpu.VMEM((OWN, N), BF),
            pltpu.SemaphoreType.DMA((6,)),
            pltpu.SemaphoreType.DMA((6,)),
            pltpu.SemaphoreType.DMA((2 * (Gather.RECV + 8) + 3 * Gather.RECV + 1,)),
        ],
        compiler_params=pltpu.CompilerParams(
            collective_id=0, has_side_effects=True, vmem_limit_bytes=48 * 1024 * 1024
        ),
    )(*args)


def solution(mesh):
    return jax.shard_map(
        body,
        mesh=mesh,
        in_specs=(
            P("row", "col"),
            P("row", "col"),
            P("row", "col"),
            P(None, "row", "col"),
            P(None, ("row", "col"), None),
            P(("row", "col")),
        ),
        out_specs=(P(("row", "col"), None), P(None, ("row", "col"))),
        check_vma=False,
    )
```

```python
import jax
import jax.numpy as jnp
from jax import lax
from jax.experimental import pallas as pl
from jax.experimental.pallas import tpu as pltpu
from jax.sharding import PartitionSpec as P

MESH = pl.DeviceIdType.MESH
BF, F32 = jnp.bfloat16, jnp.float32
BS = 64
ATOM_DEV = 4
N, OWN = 4096, 32
TALL, SLIM = 512, 256
ROWS, WIDE = 256, 512
PLANE, ROW = 16, 8


class Place:
    def __init__(self):
        row, col = lax.axis_index("row"), lax.axis_index("col")
        self.row, self.col = row, col
        self.zl = col // 8
        self.x, self.y, self.z, self.k = (col // 2) % 4, row // 2, (row % 2) * 2 + col // 8, col % 2
        self.own = self.x * 2 + self.k

    def at(self, x, y, z, k):
        return (y * 2 + z // 2, (z % 2) * 8 + x * 2 + k)

    def by(self, dx=0, dy=0, dz=0, dk=0):
        return self.at((self.x + dx) % 4, (self.y + dy) % 4, (self.z + dz) % 4, (self.k + dk) % 2)

    def partner(self):
        return (self.row, (self.col + 8) % 16)

    def line(self, dx, dk=0):
        return (self.x + dx) % 4 * 2 + (self.k + dk) % 2


class Copies:
    def __init__(self, me, send_sems, recv_sems):
        self.send_sems, self.recv_sems, self.any = send_sems, recv_sems, me.by(dx=1)

    def make(self, src, dst, send, recv, device):
        return pltpu.make_async_remote_copy(
            src_ref=src,
            dst_ref=dst,
            send_sem=self.send_sems.at[send],
            recv_sem=self.recv_sems.at[recv],
            device_id=device,
            device_id_type=MESH,
        )

    def send(self, src, dst, send, recv, device):
        self.make(src, dst, send, recv, device).start()

    def arrive(self, ref, recv):
        self.make(ref, ref, 0, recv, self.any).wait_recv()

    def sent(self, ref, send):
        self.make(ref, ref, send, 0, self.any).wait_send()


def new_piece(buf):
    def piece(y, z, t, lo, size):
        start = (y * 4 + z) * ROWS + t * (ROWS // 2) + lo
        return buf.at[pl.ds(pl.multiple_of(start, 64), size)]

    return piece


def old_piece(buf, first, rows):
    def piece(y, z, t, lo, size):
        start = (y * 2 + z // 2) * TALL + first + t * rows + lo
        return buf.at[
            pl.ds(pl.multiple_of(start, 64), size), pl.ds(pl.multiple_of(z % 2 * SLIM, SLIM), SLIM)
        ]

    return piece


class Plane:
    def __init__(self, cp, me, buf, piece, rows, width, send, recv):
        self.cp, self.me, self.buf, self.piece = cp, me, buf, piece
        self.rows, self.send, self.recv = rows, send, recv
        self.equal = rows * width // WIDE

    def ref(self, t, i, j, lo=0, size=None):
        back = (i, j) if t == 0 else (j, i)
        y, z = (self.me.y + 4 - back[0]) % 4, (self.me.z + 4 - back[1]) % 4
        return self.piece(y, z, t, lo, self.rows if size is None else size)

    def put(self, t, i, j, axis, d, sem, lo=0, size=None):
        ref = self.ref(t, i, j, lo, size)
        device = self.me.by(dy=d) if axis == t else self.me.by(dz=d)
        self.cp.send(ref, ref, self.send, self.recv + sem, device)

    def got(self, sem, pieces=1):
        self.cp.arrive(self.buf.at[: pieces * self.equal], self.recv + sem)

    def start(self):
        for t in range(2):
            self.put(t, 0, 0, 0, 1, 7 * t)
            self.put(t, 0, 0, 0, 3, 7 * t + 1)
        for t in range(2):
            self.put(t, 0, 0, 1, 1, 7 * t + 3)
            self.put(t, 0, 0, 1, 3, 7 * t + 3)

    def first_ring(self):
        half = self.rows // 2
        for t in range(2):
            self.got(7 * t)
            self.put(t, 1, 0, 0, 1, 7 * t + 2, 0, half)
            self.got(7 * t + 1)
            self.put(t, 3, 0, 0, 3, 7 * t + 2, half, half)
        for t in range(2):
            self.put(t, 1, 0, 1, 1, 14)
            self.put(t, 1, 0, 1, 3, 7 * t + 4)
            self.put(t, 3, 0, 1, 1, 7 * t + 5)
            self.put(t, 3, 0, 1, 3, 14)

    def second_own(self):
        for t in range(2):
            self.got(7 * t + 3, 2)
            self.put(t, 0, 1, 1, 1, 15)

    def first_far(self):
        for t in range(2):
            self.got(7 * t + 2)
            self.put(t, 2, 0, 1, 1, 14)
            self.put(t, 2, 0, 1, 3, 7 * t + 6)

    def second_left(self):
        for t in range(2):
            self.got(7 * t + 4)
            self.put(t, 1, 3, 1, 3, 15)

    def second_right(self):
        for t in range(2):
            self.got(7 * t + 5)
            self.put(t, 3, 1, 1, 1, 15)

    def second_far(self):
        for t in range(2):
            self.got(7 * t + 6)
            self.put(t, 2, 3, 1, 3, 15)

    def near(self):
        self.got(14, 6)

    def far(self):
        self.got(15, 8)

    def drain(self):
        self.cp.sent(self.buf.at[: 30 * self.equal], self.send)


class Row:
    def __init__(self, cp, me, buf, send, recv):
        self.cp, self.me, self.buf, self.send, self.recv = cp, me, buf, send, recv

    def ref(self, d, dk=0, lo=0, size=ROWS):
        at = pl.multiple_of(self.me.line(4 - d, dk) * WIDE, WIDE)
        return self.buf.at[lo : lo + size, pl.ds(at, WIDE)]

    def put(self, d, to, sem, half=None, dk=0):
        ref = self.ref(d) if half is None else self.ref(d, 0, half * (ROWS // 2), ROWS // 2)
        self.cp.send(ref, ref, self.send, self.recv + sem, self.me.by(dx=to, dk=dk))

    def got(self, sem):
        self.cp.arrive(self.ref(0), self.recv + sem)

    def got_half(self, sem):
        self.cp.arrive(self.ref(0, 0, 0, ROWS // 2), self.recv + sem)

    def share(self, d):
        self.put(d, 0, 4 + d, dk=1)

    def start(self):
        self.put(0, 1, 0, 0)
        self.put(0, 3, 1, 1)
        self.put(0, 1, 2, 1)
        self.put(0, 3, 2, 0)
        self.share(0)

    def pass_on(self):
        self.got_half(0)
        self.put(1, 1, 3, 0)
        self.got_half(1)
        self.put(3, 3, 3, 1)

    def near(self):
        self.got(2)
        self.share(1)
        self.share(3)

    def far(self):
        self.got(3)
        self.share(2)

    def shared(self, *tiles):
        for d in tiles:
            self.got(4 + d)

    def drain(self):
        self.cp.sent(self.buf.at[:, : 7 * WIDE], self.send)


def dot(a, b):
    return jnp.dot(a, b, preferred_element_type=F32)


def block_k(b, zl):
    return pl.ds(pl.multiple_of((zl * 8 + b) * ROWS, ROWS), ROWS)


class Product:
    def __init__(self, left, right):
        self.left, self.right, self.total = left, right, None

    def add(self, b, zl):
        at = pl.ds(pl.multiple_of(b * WIDE + zl * SLIM, SLIM), SLIM)
        term = dot(self.left[:, at], self.right[block_k(b, zl)])
        self.total = term if self.total is None else self.total + term

    def tiles(self, me, dk, *ds):
        for d in ds:
            for zl in range(2):
                self.add(me.line(4 - d, dk), zl)


def mask_row(blocks, i):
    count = blocks.shape[0]
    lane = lax.broadcasted_iota(jnp.int32, (1, count * BS), 1) // BS
    row = jnp.zeros((1, count * BS), F32)
    for j in range(count):
        row = jnp.where(lane == j, blocks[j : j + 1, i : i + 1], row)
    return row


def kernel(
    hamil_hbm, guess_hbm, pattern_hbm, filters_hbm, deriv_hbm, atoms_hbm,
    energy_out, forces_out,
    hamil, guess, pattern, filters, deriv, atoms,
    rowp, colp, srow, hcol, square, etile, eall, others, load_sems, send_sems, recv_sems,
):
    me = Place()
    cp = Copies(me, send_sems, recv_sems)
    peers = [me.by(dx=dx, dk=dk) for dx in range(4) for dk in range(2)][1:]
    peers += [me.by(dy=1), me.by(dy=3), me.by(dz=1), me.by(dz=3)]
    barrier = pltpu.get_barrier_semaphore()
    for peer in peers:
        pl.semaphore_signal(barrier, inc=1, device_id=peer, device_id_type=MESH)

    pairs = [(pattern_hbm, pattern), (guess_hbm, guess), (hamil_hbm, hamil)]
    pairs += [(filters_hbm, filters), (deriv_hbm, deriv), (atoms_hbm, atoms)]
    loads = [pltpu.make_async_copy(a, b, load_sems.at[i]) for i, (a, b) in enumerate(pairs)]
    for load in loads:
        load.start()
    for load in loads[:4]:
        load.wait()

    tall = pl.ds(pl.multiple_of(me.row * TALL, TALL), TALL)
    slim = pl.ds(pl.multiple_of(me.zl * SLIM, SLIM), SLIM)
    own_guess, own_ham = colp.at[0].at[tall, slim], hcol.at[tall, slim]
    kept = pattern[...].astype(F32)
    for i in range(TALL // BS):
        part = slice(i * BS, (i + 1) * BS)
        keep = mask_row(kept, i)
        here = me.row * TALL + i * BS + lax.broadcasted_iota(jnp.int32, (BS, SLIM), 0)
        there = me.col * SLIM + lax.broadcasted_iota(jnp.int32, (BS, SLIM), 1)
        half = jnp.where(here == there, 0.5, 0.0).astype(F32)
        own_guess[part] = ((half + guess[part].astype(F32)) * keep).astype(BF)
        own_ham[part] = jnp.where(keep > 0, hamil[part].astype(F32), 0.0).astype(BF)
    pl.semaphore_wait(barrier, len(peers))

    mine = pl.ds(pl.multiple_of((me.y * 4 + me.z) * ROWS, ROWS), ROWS)
    own_rows = pl.ds(pl.multiple_of(me.own * WIDE, WIDE), WIDE)
    planes = 2 * ROW
    filters_sem, energy_sem = planes + 4 * PLANE, planes + 4 * PLANE + 1

    def early(product):
        for dy in (0, 1, 3):
            for dz in (0, 1, 3):
                add_block(product, dy, dz)

    def late(product):
        for d in range(4):
            add_block(product, d, 2)
        for d in (0, 1, 3):
            add_block(product, 2, d)

    def add_block(product, dy, dz):
        r = (me.y + 4 - dy) % 4 * 4 + (me.z + 4 - dz) % 4
        product.add(r % 8, r // 8)

    cp.send(filters, others, 6, filters_sem, me.partner())
    for step in range(3):
        panel = colp.at[step % 2]
        piece = old_piece(panel, 0, TALL // 2) if step == 0 else new_piece(panel)
        shape = (TALL // 2, SLIM) if step == 0 else (ROWS // 2, WIDE)
        plane = Plane(cp, me, panel, piece, *shape, 2 + step % 2, planes + step % 2 * PLANE)
        rows = Row(cp, me, rowp, 0, 0)
        inner = Row(cp, me, srow, 1, ROW)
        second = Product(srow, panel)
        if step < 2:
            first = Product(rowp, panel)
            plane.start()
            if step == 0:
                plane.first_ring()
                plane.second_own()
                rowp[:, own_rows] = panel[mine]
                rows.start()
                plane.first_far()
                plane.second_left()
                plane.second_right()
                rows.pass_on()
                rows.near()
                plane.second_far()
                rows.far()
            else:
                rows.start()
                plane.first_ring()
                rows.pass_on()
                plane.second_own()
                rows.near()
                plane.first_far()
                rows.far()
                plane.second_left()
                plane.second_right()
                plane.second_far()
            rows.shared(0, 1, 3, 2)
            plane.near()
            if step == 1:
                early(first)
            plane.far()
            if step == 0:
                early(first)
            late(first)
            rows.drain()
            plane.drain()
            srow[:, own_rows] = first.total.astype(BF)
            ham_piece = old_piece(hcol, step * (TALL // 2), TALL // 4)
            ham = Plane(cp, me, hcol, ham_piece, TALL // 4, SLIM, 4 + step, planes + (2 + step) * PLANE)
            inner.start()
            ham.start()
            square[...] = first.total
            second.tiles(me, 0, 0)
            ham.first_ring()
            inner.pass_on()
            ham.second_own()
            ham.first_far()
            inner.shared(0)
            second.tiles(me, 1, 0)
            inner.near()
            second.tiles(me, 0, 1, 3)
            ham.second_left()
            inner.far()
            ham.second_right()
            inner.shared(1, 3)
            second.tiles(me, 1, 1, 3)
            second.tiles(me, 0, 2)
            ham.second_far()
            inner.shared(2)
            second.tiles(me, 1, 2)
            inner.drain()
            if step == 0:
                cp.arrive(others, filters_sem)
            blocks = [filters[step].astype(F32), others[step].astype(F32)]
            keep = [jnp.where(me.zl == 0, m[:, :4], m[:, 4:]) for m in blocks]
            left = jnp.where(me.zl == 0, keep[0], keep[1])
            right = jnp.where(me.zl == 0, keep[1], keep[0])
            after = colp.at[(step + 1) % 2]
            own_piece = after.at[mine]
            own_block = rowp.at[:, own_rows]
            for i in range(ROWS // BS):
                part = slice(i * BS, (i + 1) * BS)
                mask = jnp.concatenate([mask_row(left, i), mask_row(right, i)], axis=1)
                dens = (mask * (3.0 * square[part] - 2.0 * second.total[part])).astype(BF)
                own_piece[part] = dens
                own_block[part] = dens
            ham.near()
            ham.far()
            ham.drain()
        else:
            first = Product(rowp, hcol)
            rows.start()
            plane.start()
            rows.pass_on()
            plane.first_ring()
            first.tiles(me, 0, 0)
            rows.shared(0)
            first.tiles(me, 1, 0)
            plane.second_own()
            rows.near()
            first.tiles(me, 0, 1, 3)
            plane.first_far()
            rows.far()
            rows.shared(1, 3)
            first.tiles(me, 1, 1, 3)
            first.tiles(me, 0, 2)
            plane.second_left()
            rows.shared(2)
            first.tiles(me, 1, 2)
            srow[:, own_rows] = first.total.astype(BF)
            inner.start()
            plane.second_right()
            plane.second_far()
            inner.pass_on()
            plane.near()
            inner.near()
            plane.far()
            second.tiles(me, 0, 0, 1, 3)
            inner.shared(0)
            second.tiles(me, 1, 0)
            inner.far()
            inner.shared(1, 3)
            second.tiles(me, 1, 1, 3)
            second.tiles(me, 0, 2)
            inner.shared(2)
            second.tiles(me, 1, 2)
            etile[...] = second.total.astype(BF)
            rows.drain()
            plane.drain()
            inner.drain()

    rels = [(dx, dk) for dx in (2, 1, 3, 0) for dk in range(2)][:-2] + [(0, 1)]
    for dx, dk in rels:
        src = etile.at[pl.ds(pl.multiple_of(me.line(dx, dk) * OWN, OWN), OWN)]
        cp.send(src, eall.at[:, own_rows], 0, energy_sem, me.by(dx=dx, dk=dk))
    eall[:, own_rows] = etile[pl.ds(pl.multiple_of(me.own * OWN, OWN), OWN)]
    same = lax.broadcasted_iota(jnp.int32, (OWN, OWN), 0) == lax.broadcasted_iota(jnp.int32, (OWN, OWN), 1)
    loads[4].wait()
    loads[5].wait()
    atom_of = jnp.sum(jnp.where(same, atoms[...].astype(F32), 0.0), axis=1, keepdims=True)
    cp.sent(filters, 6)
    cp.arrive(eall.at[:, : 7 * WIDE], energy_sem)
    for b in range(8):
        for zl in range(2):
            energy_out[:, (zl * 8 + b) * SLIM : (zl * 8 + b + 1) * SLIM] = eall[
                :, b * WIDE + zl * SLIM : b * WIDE + (zl + 1) * SLIM
            ]
    wide = energy_out[...].astype(F32)
    line = lax.broadcasted_iota(jnp.int32, (3, ATOM_DEV), 0)
    lane = lax.broadcasted_iota(jnp.int32, (3, ATOM_DEV), 1)
    forces = jnp.zeros((3, ATOM_DEV), F32)
    for axis in range(3):
        per_row = jnp.sum(deriv[axis].astype(F32) * wide, axis=1, keepdims=True)
        for atom in range(ATOM_DEV):
            force = jnp.sum(jnp.where(atom_of == atom, per_row, 0.0))
            forces = jnp.where((line == axis) & (lane == atom), force, forces)
    forces_out[...] = forces
    cp.sent(eall.at[:, : 7 * WIDE], 0)


def body(hamil, guess, pattern, filters, deriv, atom_of_row):
    args = (hamil, guess, pattern.T, filters.transpose(0, 2, 1), deriv, atom_of_row.reshape(1, OWN))
    vmem = pl.BlockSpec(memory_space=pltpu.VMEM)
    return pl.pallas_call(
        kernel,
        out_shape=(
            jax.ShapeDtypeStruct((OWN, N), BF),
            jax.ShapeDtypeStruct((3, ATOM_DEV), F32),
        ),
        in_specs=[pl.BlockSpec(memory_space=pl.ANY)] * 6,
        out_specs=(vmem, vmem),
        scratch_shapes=[pltpu.VMEM(arg.shape, arg.dtype) for arg in args]
        + [
            pltpu.VMEM((ROWS, N), BF),
            pltpu.VMEM((2, N, WIDE), BF),
            pltpu.VMEM((ROWS, N), BF),
            pltpu.VMEM((N, WIDE), BF),
            pltpu.VMEM((ROWS, WIDE), F32),
            pltpu.VMEM((ROWS, WIDE), BF),
            pltpu.VMEM((OWN, N), BF),
            pltpu.VMEM(args[3].shape, args[3].dtype),
            pltpu.SemaphoreType.DMA((6,)),
            pltpu.SemaphoreType.DMA((7,)),
            pltpu.SemaphoreType.DMA((2 * ROW + 4 * PLANE + 2,)),
        ],
        compiler_params=pltpu.CompilerParams(
            collective_id=0, has_side_effects=True, vmem_limit_bytes=60 * 1024 * 1024
        ),
    )(*args)


def solution(mesh):
    return jax.shard_map(
        body,
        mesh=mesh,
        in_specs=(
            P("row", "col"),
            P("row", "col"),
            P("row", "col"),
            P(None, "row", "col"),
            P(None, ("row", "col"), None),
            P(("row", "col")),
        ),
        out_specs=(P(("row", "col"), None), P(None, ("row", "col"))),
        check_vma=False,
    )
```

```python
import jax
import jax.numpy as jnp
from jax import lax
from jax.experimental import pallas as pl
from jax.experimental.pallas import tpu as pltpu
from jax.sharding import PartitionSpec as P

MESH = pl.DeviceIdType.MESH
BF, F32 = jnp.bfloat16, jnp.float32
BS = 64
ATOM_DEV = 4
N, OWN = 4096, 32
TALL, SLIM = 512, 256
ROWS, WIDE = 256, 512
CHUNKS = 4
CHUNK = ROWS // CHUNKS
PLANE, ROW = 16, 5


class Place:
    def __init__(self):
        row, col = lax.axis_index("row"), lax.axis_index("col")
        self.row, self.col = row, col
        self.zl = col // 8
        self.x, self.y, self.z, self.k = (col // 2) % 4, row // 2, (row % 2) * 2 + col // 8, col % 2
        self.own = self.x * 2 + self.k

    def at(self, x, y, z, k):
        return (y * 2 + z // 2, (z % 2) * 8 + x * 2 + k)

    def by(self, dx=0, dy=0, dz=0, dk=0):
        return self.at((self.x + dx) % 4, (self.y + dy) % 4, (self.z + dz) % 4, (self.k + dk) % 2)

    def partner(self):
        return (self.row, (self.col + 8) % 16)

    def line(self, dx, dk=0):
        return (self.x + dx) % 4 * 2 + (self.k + dk) % 2


class Copies:
    def __init__(self, me, send_sems, recv_sems):
        self.send_sems, self.recv_sems, self.any = send_sems, recv_sems, me.by(dx=1)

    def make(self, src, dst, send, recv, device):
        return pltpu.make_async_remote_copy(
            src_ref=src,
            dst_ref=dst,
            send_sem=self.send_sems.at[send],
            recv_sem=self.recv_sems.at[recv],
            device_id=device,
            device_id_type=MESH,
        )

    def send(self, src, dst, send, recv, device):
        self.make(src, dst, send, recv, device).start()

    def arrive(self, ref, recv):
        self.make(ref, ref, 0, recv, self.any).wait_recv()

    def sent(self, ref, send):
        self.make(ref, ref, send, 0, self.any).wait_send()


def chunk_piece(buf, first):
    def piece(y, z, t, lo, size):
        start = (y * 4 + z) * ROWS + (first + t) * CHUNK + lo
        return buf.at[pl.ds(pl.multiple_of(start, 32), size)]

    return piece


def tall_piece(buf, first, rows, swap=0):
    def piece(y, z, t, lo, size):
        start = (y * 2 + z // 2) * TALL + first + (t + swap * z) % 2 * rows + lo
        return buf.at[
            pl.ds(pl.multiple_of(start, 64), size), pl.ds(pl.multiple_of(z % 2 * SLIM, SLIM), SLIM)
        ]

    return piece


class Plane:
    def __init__(self, cp, me, buf, piece, rows, width, send, recv):
        self.cp, self.me, self.buf, self.piece = cp, me, buf, piece
        self.rows, self.send, self.recv = rows, send, recv
        self.equal = rows * width // WIDE

    def ref(self, t, i, j, lo=0, size=None):
        back = (i, j) if t == 0 else (j, i)
        y, z = (self.me.y + 4 - back[0]) % 4, (self.me.z + 4 - back[1]) % 4
        return self.piece(y, z, t, lo, self.rows if size is None else size)

    def put(self, t, i, j, axis, d, sem, lo=0, size=None):
        ref = self.ref(t, i, j, lo, size)
        device = self.me.by(dy=d) if axis == t else self.me.by(dz=d)
        self.cp.send(ref, ref, self.send, self.recv + sem, device)

    def got(self, sem, pieces=1):
        self.cp.arrive(self.buf.at[: pieces * self.equal], self.recv + sem)

    def start_first(self, t):
        self.put(t, 0, 0, 0, 1, 7 * t)
        self.put(t, 0, 0, 0, 3, 7 * t + 1)

    def start_second(self, t):
        self.put(t, 0, 0, 1, 1, 7 * t + 3)
        self.put(t, 0, 0, 1, 3, 7 * t + 3)

    def start(self, *ts):
        for t in ts:
            self.start_first(t)
        for t in ts:
            self.start_second(t)

    def first_ring(self, t):
        half = self.rows // 2
        self.got(7 * t)
        self.put(t, 1, 0, 0, 1, 7 * t + 2, 0, half)
        self.got(7 * t + 1)
        self.put(t, 3, 0, 0, 3, 7 * t + 2, half, half)
        self.put(t, 1, 0, 1, 1, 14)
        self.put(t, 1, 0, 1, 3, 7 * t + 4)
        self.put(t, 3, 0, 1, 1, 7 * t + 5)
        self.put(t, 3, 0, 1, 3, 14)

    def second_own(self, t):
        self.got(7 * t + 3, 2)
        self.put(t, 0, 1, 1, 1, 15)

    def first_far(self, t):
        self.got(7 * t + 2)
        self.put(t, 2, 0, 1, 1, 14)
        self.put(t, 2, 0, 1, 3, 7 * t + 6)

    def second_left(self, t):
        self.got(7 * t + 4)
        self.put(t, 1, 3, 1, 3, 15)

    def second_right(self, t):
        self.got(7 * t + 5)
        self.put(t, 3, 1, 1, 1, 15)

    def second_far(self, t):
        self.got(7 * t + 6)
        self.put(t, 2, 3, 1, 3, 15)

    def near(self):
        self.got(14, 6)

    def far(self):
        self.got(15, 8)

    def drain(self):
        self.cp.sent(self.buf.at[: 30 * self.equal], self.send)


class Row:
    def __init__(self, cp, me, buf, send, recv, lo=0, size=CHUNK):
        self.cp, self.me, self.buf, self.send, self.recv = cp, me, buf, send, recv
        self.lo, self.size = lo, size

    def put(self, d, to, sem, dk=0):
        at = pl.multiple_of(self.me.line(4 - d) * WIDE, WIDE)
        ref = self.buf.at[self.lo : self.lo + self.size, pl.ds(at, WIDE)]
        self.cp.send(ref, ref, self.send, self.recv + sem, self.me.by(dx=to, dk=dk))

    def got(self, sem, tiles=1):
        self.cp.arrive(self.buf.at[: self.size, : tiles * WIDE], self.recv + sem)

    def start(self):
        self.put(0, 1, 0)
        self.put(0, 3, 0)
        self.put(0, 2, 1)
        self.put(0, 0, 2, dk=1)

    def arrive(self):
        self.got(0, 2)
        self.put(1, 0, 3, dk=1)
        self.put(3, 0, 3, dk=1)
        self.got(1)
        self.put(2, 0, 4, dk=1)

    def shared_own(self):
        self.got(2)

    def shared(self):
        self.got(3, 2)
        self.got(4)


def dot(a, b):
    return jnp.dot(a, b, preferred_element_type=F32)


def block_k(b, zl):
    return pl.ds(pl.multiple_of((zl * 8 + b) * ROWS, ROWS), ROWS)


class Product:
    def __init__(self, left, right, lo=0, size=ROWS):
        self.left, self.right, self.rows, self.total = left, right, slice(lo, lo + size), None

    def add(self, b, zl):
        at = pl.ds(pl.multiple_of(b * WIDE + zl * SLIM, SLIM), SLIM)
        term = dot(self.left[self.rows, at], self.right[block_k(b, zl)])
        self.total = term if self.total is None else self.total + term

    def tiles(self, me, dk, *ds):
        for d in ds:
            for zl in range(2):
                self.add(me.line(4 - d, dk), zl)

    def blocks(self, me, pairs):
        for dy, dz in pairs:
            r = (me.y + 4 - dy) % 4 * 4 + (me.z + 4 - dz) % 4
            self.add(r % 8, r // 8)


EARLY = [(dy, dz) for dy in (0, 1, 3) for dz in (0, 1, 3)]
LATE = [(d, 2) for d in range(4)] + [(2, d) for d in (0, 1, 3)]


def mask_row(blocks, i):
    count = blocks.shape[0]
    lane = lax.broadcasted_iota(jnp.int32, (1, count * BS), 1) // BS
    row = jnp.zeros((1, count * BS), F32)
    for j in range(count):
        row = jnp.where(lane == j, blocks[j : j + 1, i : i + 1], row)
    return row


def kernel(
    hamil_hbm, guess_hbm, pattern_hbm, filters_hbm, deriv_hbm, atoms_hbm,
    energy_out, forces_out,
    hamil, guess, pattern, filters, deriv, atoms,
    rowp, colp, srow, grow, hcol, square, etile, eall, others, load_sems, send_sems, recv_sems,
):
    me = Place()
    cp = Copies(me, send_sems, recv_sems)
    peers = [me.by(dx=dx, dk=dk) for dx in range(4) for dk in range(2)][1:]
    peers += [me.by(dy=1), me.by(dy=3), me.by(dz=1), me.by(dz=3)]
    barrier = pltpu.get_barrier_semaphore()
    for peer in peers:
        pl.semaphore_signal(barrier, inc=1, device_id=peer, device_id_type=MESH)

    pairs = [(pattern_hbm, pattern), (guess_hbm, guess), (hamil_hbm, hamil)]
    pairs += [(filters_hbm, filters), (deriv_hbm, deriv), (atoms_hbm, atoms)]
    loads = [pltpu.make_async_copy(a, b, load_sems.at[i]) for i, (a, b) in enumerate(pairs)]
    for load in loads:
        load.start()
    for load in loads[:4]:
        load.wait()

    tall = pl.ds(pl.multiple_of(me.row * TALL, TALL), TALL)
    slim = pl.ds(pl.multiple_of(me.zl * SLIM, SLIM), SLIM)
    own_guess, own_ham = colp.at[0].at[tall, slim], hcol.at[tall, slim]
    kept = pattern[...].astype(F32)
    for i in range(TALL // BS):
        part = slice(i * BS, (i + 1) * BS)
        keep = mask_row(kept, i)
        here = me.row * TALL + i * BS + lax.broadcasted_iota(jnp.int32, (BS, SLIM), 0)
        there = me.col * SLIM + lax.broadcasted_iota(jnp.int32, (BS, SLIM), 1)
        half = jnp.where(here == there, 0.5, 0.0).astype(F32)
        own_guess[part] = ((half + guess[part].astype(F32)) * keep).astype(BF)
        own_ham[part] = jnp.where(keep > 0, hamil[part].astype(F32), 0.0).astype(BF)
    pl.semaphore_wait(barrier, len(peers))

    mine = pl.ds(pl.multiple_of((me.y * 4 + me.z) * ROWS, ROWS), ROWS)
    own_rows = pl.ds(pl.multiple_of(me.own * WIDE, WIDE), WIDE)
    chunk = [slice(c * CHUNK, (c + 1) * CHUNK) for c in range(CHUNKS)]
    row_sems = CHUNKS * ROW
    planes = 3 * row_sems
    plane_sems = [[planes], [planes + PLANE, planes + 2 * PLANE], [planes, planes + 3 * PLANE]]
    ham_sems = [planes + 4 * PLANE, planes + 5 * PLANE]
    filters_sem, energy_sem = planes + 6 * PLANE, planes + 6 * PLANE + 1

    def row_chunks(buf, send, group):
        return [Row(cp, me, buf, send, group * row_sems + c * ROW, c * CHUNK) for c in range(CHUNKS)]

    def drain_rows(buf, send):
        cp.sent(buf.at[:, : 7 * WIDE], send)

    cp.send(filters, others, 6, filters_sem, me.partner())
    panel = colp.at[0]
    plane = Plane(cp, me, panel, tall_piece(panel, 0, TALL // 2, 1), TALL // 2, SLIM, 2, plane_sems[0][0])
    rows = Row(cp, me, rowp, 0, 0, 0, ROWS)
    plane.start(0, 1)
    plane.first_ring(1)
    rowp[:, own_rows] = panel[mine]
    rows.start()
    plane.first_ring(0)
    for stage in (plane.second_own, plane.first_far, plane.second_left, plane.second_right, plane.second_far):
        stage(0)
        stage(1)
    rows.arrive()
    plane.near()
    rows.shared_own()
    rows.shared()
    first = Product(rowp, panel)
    first.blocks(me, EARLY)
    plane.far()
    plane.drain()
    cp.arrive(others, filters_sem)

    for step in range(2):
        drain_rows(rowp, 0)
        ham_piece = tall_piece(hcol, step * (TALL // 2), TALL // 4)
        ham = Plane(cp, me, hcol, ham_piece, TALL // 4, SLIM, 4 + step, ham_sems[step])
        inner = row_chunks(srow, 1, 1)
        thirds = []
        for c in range(CHUNKS):
            tail = Product(rowp, panel, c * CHUNK, CHUNK)
            tail.total = first.total[chunk[c]]
            tail.blocks(me, LATE)
            srow[chunk[c], own_rows] = tail.total.astype(BF)
            inner[c].start()
            if c == 0:
                ham.start(0, 1)
            square[chunk[c]] = tail.total
            thirds.append(Product(srow, panel, c * CHUNK, CHUNK))

        after = colp.at[(step + 1) % 2]
        own_piece, own_block = after.at[mine], rowp.at[:, own_rows]
        first_sem, second_sem = plane_sems[step + 1]
        pair = [
            Plane(cp, me, after, chunk_piece(after, 0), CHUNK, WIDE, 2 + (step + 1) % 2, first_sem),
            Plane(cp, me, after, chunk_piece(after, 2), CHUNK, WIDE, 2 + (step + 1) % 2, second_sem),
        ]
        rows = row_chunks(rowp, 0, 0)
        blocks = [filters[step].astype(F32), others[step].astype(F32)]
        keep = [jnp.where(me.zl == 0, m[:, :4], m[:, 4:]) for m in blocks]
        left = jnp.where(me.zl == 0, keep[0], keep[1])
        right = jnp.where(me.zl == 0, keep[1], keep[0])

        def finish(c):
            third = thirds[c]
            third.tiles(me, 0, 0)
            inner[c].shared_own()
            third.tiles(me, 1, 0)
            inner[c].arrive()
            third.tiles(me, 0, 1, 3, 2)
            inner[c].shared()
            third.tiles(me, 1, 1, 3, 2)
            mask = jnp.concatenate([mask_row(left, c), mask_row(right, c)], axis=1)
            dens = (mask * (3.0 * square[chunk[c]] - 2.0 * third.total)).astype(BF)
            own_piece[chunk[c]] = dens
            own_block[chunk[c]] = dens
            pair[c // 2].start(c % 2)
            if c == CHUNKS - 1:
                drain_rows(srow, 1)
            rows[c].start()

        def both(stage):
            stage(0)
            stage(1)

        both(ham.first_ring)
        both(ham.second_own)
        finish(0)
        both(ham.first_far)
        finish(1)
        both(ham.second_left)
        both(ham.second_right)
        pair[0].first_ring(0)
        pair[0].second_own(0)
        finish(2)
        both(ham.second_far)
        pair[0].first_ring(1)
        pair[0].second_own(1)
        finish(3)
        pair[0].first_far(0)
        pair[0].second_left(0)
        ham.near()
        ham.far()

        panel = after
        if step == 0:
            rows[0].arrive()
            pair[0].second_right(0)
            pair[1].first_ring(0)
            pair[1].second_own(0)
            pair[0].first_far(1)
            pair[0].second_left(1)
            rows[1].arrive()
            pair[0].second_far(0)
            pair[0].second_right(1)
            pair[1].first_ring(1)
            pair[1].second_own(1)
            pair[1].first_far(0)
            rows[2].arrive()
            pair[1].second_left(0)
            pair[0].second_far(1)
            pair[1].second_right(0)
            pair[1].first_far(1)
            pair[1].second_left(1)
            rows[3].arrive()
            pair[1].second_far(0)
            pair[1].second_right(1)
            pair[1].second_far(1)
            for row in rows:
                row.shared_own()
                row.shared()
            pair[0].near()
            pair[0].far()
            pair[1].near()
            first = Product(rowp, panel)
            first.blocks(me, EARLY)
            pair[1].far()
        else:
            energy_rows = row_chunks(grow, 7, 2)

            def inward(c):
                rows[c].shared_own()
                rows[c].shared()
                part = Product(rowp, hcol, c * CHUNK, CHUNK)
                part.tiles(me, 0, 0, 1, 3, 2)
                part.tiles(me, 1, 0, 1, 3, 2)
                grow[chunk[c], own_rows] = part.total.astype(BF)
                energy_rows[c].start()

            rows[0].arrive()
            pair[0].second_right(0)
            pair[1].first_ring(0)
            inward(0)
            pair[1].second_own(0)
            pair[0].first_far(1)
            pair[0].second_left(1)
            rows[1].arrive()
            pair[0].second_far(0)
            pair[0].second_right(1)
            pair[1].first_ring(1)
            inward(1)
            pair[1].second_own(1)
            pair[1].first_far(0)
            rows[2].arrive()
            pair[1].second_left(0)
            pair[0].second_far(1)
            pair[1].second_right(0)
            inward(2)
            pair[1].first_far(1)
            pair[1].second_left(1)
            rows[3].arrive()
            pair[1].second_far(0)
            energy_rows[0].arrive()
            inward(3)
            pair[1].second_right(1)
            pair[1].second_far(1)
            energy_rows[1].arrive()
            pair[0].near()
            pair[0].far()
            pair[1].near()
            energy_rows[2].arrive()
            for c in range(3):
                energy_rows[c].shared_own()
                energy_rows[c].shared()
            pair[1].far()
            upper, lower = Product(grow, panel, 0, 3 * CHUNK), Product(grow, panel, 3 * CHUNK, CHUNK)
            for dk in range(2):
                upper.tiles(me, dk, 0, 1, 3, 2)
            etile[: 3 * CHUNK] = upper.total.astype(BF)
            lower.tiles(me, 0, 0)
            energy_rows[3].shared_own()
            lower.tiles(me, 1, 0)
            energy_rows[3].arrive()
            lower.tiles(me, 0, 1, 3, 2)
            energy_rows[3].shared()
            lower.tiles(me, 1, 1, 3, 2)
            etile[3 * CHUNK :] = lower.total.astype(BF)
            drain_rows(rowp, 0)
            drain_rows(grow, 7)
        both_sent = after.at[: 60 * CHUNK]
        cp.sent(both_sent, 2 + (step + 1) % 2)
        ham.drain()

    rels = [(dx, dk) for dx in (2, 1, 3, 0) for dk in range(2)][:-2] + [(0, 1)]
    for dx, dk in rels:
        src = etile.at[pl.ds(pl.multiple_of(me.line(dx, dk) * OWN, OWN), OWN)]
        cp.send(src, eall.at[:, own_rows], 0, energy_sem, me.by(dx=dx, dk=dk))
    eall[:, own_rows] = etile[pl.ds(pl.multiple_of(me.own * OWN, OWN), OWN)]
    same = lax.broadcasted_iota(jnp.int32, (OWN, OWN), 0) == lax.broadcasted_iota(jnp.int32, (OWN, OWN), 1)
    loads[4].wait()
    loads[5].wait()
    atom_of = jnp.sum(jnp.where(same, atoms[...].astype(F32), 0.0), axis=1, keepdims=True)
    cp.sent(filters, 6)
    cp.arrive(eall.at[:, : 7 * WIDE], energy_sem)
    for b in range(8):
        for zl in range(2):
            energy_out[:, (zl * 8 + b) * SLIM : (zl * 8 + b + 1) * SLIM] = eall[
                :, b * WIDE + zl * SLIM : b * WIDE + (zl + 1) * SLIM
            ]
    wide = energy_out[...].astype(F32)
    line = lax.broadcasted_iota(jnp.int32, (3, ATOM_DEV), 0)
    lane = lax.broadcasted_iota(jnp.int32, (3, ATOM_DEV), 1)
    forces = jnp.zeros((3, ATOM_DEV), F32)
    for axis in range(3):
        per_row = jnp.sum(deriv[axis].astype(F32) * wide, axis=1, keepdims=True)
        for atom in range(ATOM_DEV):
            force = jnp.sum(jnp.where(atom_of == atom, per_row, 0.0))
            forces = jnp.where((line == axis) & (lane == atom), force, forces)
    forces_out[...] = forces
    cp.sent(eall.at[:, : 7 * WIDE], 0)


def body(hamil, guess, pattern, filters, deriv, atom_of_row):
    args = (hamil, guess, pattern.T, filters.transpose(0, 2, 1), deriv, atom_of_row.reshape(1, OWN))
    vmem = pl.BlockSpec(memory_space=pltpu.VMEM)
    return pl.pallas_call(
        kernel,
        out_shape=(
            jax.ShapeDtypeStruct((OWN, N), BF),
            jax.ShapeDtypeStruct((3, ATOM_DEV), F32),
        ),
        in_specs=[pl.BlockSpec(memory_space=pl.ANY)] * 6,
        out_specs=(vmem, vmem),
        scratch_shapes=[pltpu.VMEM(arg.shape, arg.dtype) for arg in args]
        + [
            pltpu.VMEM((ROWS, N), BF),
            pltpu.VMEM((2, N, WIDE), BF),
            pltpu.VMEM((ROWS, N), BF),
            pltpu.VMEM((ROWS, N), BF),
            pltpu.VMEM((N, WIDE), BF),
            pltpu.VMEM((ROWS, WIDE), F32),
            pltpu.VMEM((ROWS, WIDE), BF),
            pltpu.VMEM((OWN, N), BF),
            pltpu.VMEM(args[3].shape, args[3].dtype),
            pltpu.SemaphoreType.DMA((6,)),
            pltpu.SemaphoreType.DMA((8,)),
            pltpu.SemaphoreType.DMA((3 * CHUNKS * ROW + 6 * PLANE + 2,)),
        ],
        compiler_params=pltpu.CompilerParams(
            collective_id=0, has_side_effects=True, vmem_limit_bytes=60 * 1024 * 1024
        ),
    )(*args)


def solution(mesh):
    return jax.shard_map(
        body,
        mesh=mesh,
        in_specs=(
            P("row", "col"),
            P("row", "col"),
            P("row", "col"),
            P(None, "row", "col"),
            P(None, ("row", "col"), None),
            P(("row", "col")),
        ),
        out_specs=(P(("row", "col"), None), P(None, ("row", "col"))),
        check_vma=False,
    )
```

```python
import functools

import jax
import jax.numpy as jnp
from jax import lax
from jax.experimental import pallas as pl
from jax.experimental.pallas import tpu as pltpu
from jax.sharding import PartitionSpec as P

MESH = pl.DeviceIdType.MESH
BF, F32 = jnp.bfloat16, jnp.float32
BS = 64
ATOM_DEV = 4
N, OWN = 4096, 32
TALL, SLIM = 512, 256
ROWS, WIDE = 256, 512
CHUNKS = 4
CHUNK = ROWS // CHUNKS
PLANE, ROW = 16, 5


class Place:
    def __init__(self):
        row, col = lax.axis_index("row"), lax.axis_index("col")
        self.row, self.col = row, col
        self.zl = col // 8
        self.x, self.y, self.z, self.k = (col // 2) % 4, row // 2, (row % 2) * 2 + col // 8, col % 2
        self.own = self.x * 2 + self.k

    def at(self, x, y, z, k):
        return (y * 2 + z // 2, (z % 2) * 8 + x * 2 + k)

    def by(self, dx=0, dy=0, dz=0, dk=0):
        return self.at((self.x + dx) % 4, (self.y + dy) % 4, (self.z + dz) % 4, (self.k + dk) % 2)

    def partner(self):
        return (self.row, (self.col + 8) % 16)

    def line(self, dx, dk=0):
        return (self.x + dx) % 4 * 2 + (self.k + dk) % 2


class Copies:
    def __init__(self, me, send_sems, recv_sems):
        self.send_sems, self.recv_sems, self.any = send_sems, recv_sems, me.by(dx=1)

    def make(self, src, dst, send, recv, device):
        return pltpu.make_async_remote_copy(
            src_ref=src,
            dst_ref=dst,
            send_sem=self.send_sems.at[send],
            recv_sem=self.recv_sems.at[recv],
            device_id=device,
            device_id_type=MESH,
        )

    def send(self, src, dst, send, recv, device):
        self.make(src, dst, send, recv, device).start()

    def arrive(self, ref, recv):
        self.make(ref, ref, 0, recv, self.any).wait_recv()

    def sent(self, ref, send):
        self.make(ref, ref, send, 0, self.any).wait_send()


def chunk_piece(buf, first):
    def piece(y, z, t, lo, size):
        start = (y * 4 + z) * ROWS + (first + t) * CHUNK + lo
        return buf.at[pl.ds(pl.multiple_of(start, 32), size)]

    return piece


def tall_piece(buf, first, rows, swap=0):
    def piece(y, z, t, lo, size):
        start = (y * 2 + z // 2) * TALL + first + (t + swap * z) % 2 * rows + lo
        return buf.at[
            pl.ds(pl.multiple_of(start, 64), size), pl.ds(pl.multiple_of(z % 2 * SLIM, SLIM), SLIM)
        ]

    return piece


class Plane:
    def __init__(self, cp, me, buf, piece, rows, width, send, recv):
        self.cp, self.me, self.buf, self.piece = cp, me, buf, piece
        self.rows, self.send, self.recv = rows, send, recv
        self.equal = rows * width // WIDE

    def ref(self, t, i, j, lo=0, size=None):
        back = (i, j) if t == 0 else (j, i)
        y, z = (self.me.y + 4 - back[0]) % 4, (self.me.z + 4 - back[1]) % 4
        return self.piece(y, z, t, lo, self.rows if size is None else size)

    def put(self, t, i, j, axis, d, sem, lo=0, size=None):
        ref = self.ref(t, i, j, lo, size)
        device = self.me.by(dy=d) if axis == t else self.me.by(dz=d)
        self.cp.send(ref, ref, self.send, self.recv + sem, device)

    def got(self, sem, pieces=1):
        self.cp.arrive(self.buf.at[: pieces * self.equal], self.recv + sem)

    def own_first(self, t):
        self.put(t, 0, 0, 0, 1, 7 * t)
        self.put(t, 0, 0, 0, 3, 7 * t + 1)

    def own_second(self, t):
        self.put(t, 0, 0, 1, 1, 7 * t + 3)
        self.put(t, 0, 0, 1, 3, 7 * t + 3)

    def ring(self, t):
        half = self.rows // 2
        self.got(7 * t)
        self.put(t, 1, 0, 0, 1, 7 * t + 2, 0, half)
        self.got(7 * t + 1)
        self.put(t, 3, 0, 0, 3, 7 * t + 2, half, half)

    def spread(self, t):
        self.put(t, 1, 0, 1, 3, 7 * t + 4)
        self.put(t, 3, 0, 1, 1, 7 * t + 5)
        self.put(t, 1, 0, 1, 1, 14)
        self.put(t, 3, 0, 1, 3, 14)

    def own_far(self, t):
        self.got(7 * t + 3, 2)
        self.put(t, 0, 1, 1, 1, 15)

    def spread_far(self, t):
        self.got(7 * t + 2)
        self.put(t, 2, 0, 1, 3, 7 * t + 6)
        self.put(t, 2, 0, 1, 1, 14)

    def left_far(self, t):
        self.got(7 * t + 4)
        self.put(t, 1, 3, 1, 3, 15)

    def right_far(self, t):
        self.got(7 * t + 5)
        self.put(t, 3, 1, 1, 1, 15)

    def far_far(self, t):
        self.got(7 * t + 6)
        self.put(t, 2, 3, 1, 3, 15)

    def tasks(self, name):
        steps = [self.own_first, self.own_second, self.ring, self.spread, self.own_far]
        steps += [self.spread_far, self.left_far, self.right_far, self.far_far]
        out = {name + str(t) + l: functools.partial(f, t) for l, f in zip("abcdefghi", steps) for t in range(2)}
        return {**out, name + "n": self.near, name + "z": self.far}

    def near(self):
        self.got(14, 6)

    def far(self):
        self.got(15, 8)

    def drain(self):
        self.cp.sent(self.buf.at[: 30 * self.equal], self.send)


class Row:
    def __init__(self, cp, me, buf, send, recv, lo=0, size=CHUNK):
        self.cp, self.me, self.buf, self.send, self.recv = cp, me, buf, send, recv
        self.lo, self.size = lo, size

    def put(self, d, to, sem, dk=0):
        at = pl.multiple_of(self.me.line(4 - d) * WIDE, WIDE)
        ref = self.buf.at[self.lo : self.lo + self.size, pl.ds(at, WIDE)]
        self.cp.send(ref, ref, self.send, self.recv + sem, self.me.by(dx=to, dk=dk))

    def got(self, sem, tiles=1):
        self.cp.arrive(self.buf.at[: self.size, : tiles * WIDE], self.recv + sem)

    def start(self):
        self.put(0, 1, 0)
        self.put(0, 3, 0)
        self.put(0, 2, 1)
        self.put(0, 0, 2, dk=1)

    def arrive(self):
        self.got(0, 2)
        self.put(1, 0, 3, dk=1)
        self.put(3, 0, 3, dk=1)
        self.got(1)
        self.put(2, 0, 4, dk=1)

    def shared_own(self):
        self.got(2)

    def shared(self):
        self.got(3, 2)
        self.got(4)


def dot(a, b):
    return jnp.dot(a, b, preferred_element_type=F32)


def block_k(b, zl):
    return pl.ds(pl.multiple_of((zl * 8 + b) * ROWS, ROWS), ROWS)


class Product:
    def __init__(self, left, right, lo=0, size=ROWS):
        self.left, self.right, self.rows, self.total = left, right, slice(lo, lo + size), None

    def add(self, b, zl):
        at = pl.ds(pl.multiple_of(b * WIDE + zl * SLIM, SLIM), SLIM)
        term = dot(self.left[self.rows, at], self.right[block_k(b, zl)])
        self.total = term if self.total is None else self.total + term

    def tiles(self, me, dk, *ds):
        for d in ds:
            for zl in range(2):
                self.add(me.line(4 - d, dk), zl)

    def blocks(self, me, pairs):
        for dy, dz in pairs:
            r = (me.y + 4 - dy) % 4 * 4 + (me.z + 4 - dz) % 4
            self.add(r % 8, r // 8)


EARLY = [(dy, dz) for dy in (0, 1, 3) for dz in (0, 1, 3)]
LATE = [(d, 2) for d in range(4)] + [(2, d) for d in (0, 1, 3)]


def mask_row(blocks, i):
    count = blocks.shape[0]
    lane = lax.broadcasted_iota(jnp.int32, (1, count * BS), 1) // BS
    row = jnp.zeros((1, count * BS), F32)
    for j in range(count):
        row = jnp.where(lane == j, blocks[j : j + 1, i : i + 1], row)
    return row


def run(tasks, order):
    for name in order:
        tasks[name]()


ORDER_A = [
    "A0a", "A1a", "A1b", "A0b", "A0c", "A1c", "A1d", "A0d", "R", "A0e", "A0f", "A1f", "A1g", "A1e", "A0h", "A0g",
    "A1h", "A1i", "A0i", "Ra", "Rs", "An", "E", "Az",
]
ORDER_B = [
    "H1a", "H0a", "S0", "S1", "S2", "H1b", "H0b", "H1c", "H0c", "H0d", "S3", "H1d", "T0", "H0e", "H1f", "H0f", "D0",
    "P0b", "H1e", "P0a", "H1g", "H0g", "T1", "D1", "P1a", "R1", "P1b", "T2", "H1h", "H1i", "H0i", "H0h", "D2",
    "Q0b", "Q0a", "T3", "P0c", "P1c", "P1d", "D3", "Q1a", "P0d", "Hz", "R0", "R3", "Q1b", "P0f", "R2", "Q0c", "Q1c",
    "P1f", "Q0d", "P1g", "Q1d", "Q0f", "P0i", "P0g", "P0e", "Q1e", "Q0e", "P0h", "P1e", "Ra3", "Q1f", "P1i", "Q0h",
    "P1h", "Ra2", "Rs3", "Q1g", "Ra0", "Q0g", "Ra1", "Pn", "Q0i", "Q1i", "Q1h", "Qn", "Rs1", "Pz", "Rs0", "Rs2",
    "E", "Hn", "Qz",
]
ORDER_C = [
    "S0", "H1a", "H0a", "S1", "S2", "H0b", "S3", "H1b", "H1c", "H0c", "H0d", "H1d", "T0", "H0e", "H1f", "H0f", "D0",
    "T1", "H0g", "R0", "P0a", "H1g", "P0b", "D1", "P1b", "P1a", "H1h", "H0h", "T2", "R1", "H0i", "D2", "Q0a", "H1i",
    "Q0b", "T3", "H1e", "P0c", "R2", "D3", "Q1a", "P1c", "Q1b", "R3", "Q0c", "Ra0", "Hn", "P1d", "Q0d", "Rs0", "Hz",
    "G0", "Q1c", "P0f", "Ra1", "P0e", "Q1d", "Ra2", "Rs1", "P1f", "P0d", "G1", "Q1f", "P1g", "Q0h", "Q1e", "Q0e",
    "Rs2", "Q0f", "P1e", "P0i", "G2", "Q0g", "Ra3", "P1h", "Q1g", "Rs3", "P0g", "Q1h", "P1i", "P0h", "Q1i", "Q0i",
    "G3", "La0", "La1", "Ls0", "La2", "Ls1", "Pn", "Qn", "Ls2", "Pz", "Qz", "U", "La3", "Ls3", "V",
]


def kernel(
    hamil_hbm, guess_hbm, pattern_hbm, filters_hbm, deriv_hbm, atoms_hbm,
    energy_out, forces_out,
    hamil, guess, pattern, filters, deriv, atoms,
    rowp, colp, srow, grow, hcol, square, etile, eall, others, load_sems, send_sems, recv_sems,
):
    me = Place()
    cp = Copies(me, send_sems, recv_sems)
    peers = [me.by(dx=dx, dk=dk) for dx in range(4) for dk in range(2)][1:]
    peers += [me.by(dy=1), me.by(dy=3), me.by(dz=1), me.by(dz=3)]
    barrier = pltpu.get_barrier_semaphore()
    for peer in peers:
        pl.semaphore_signal(barrier, inc=1, device_id=peer, device_id_type=MESH)

    pairs = [(pattern_hbm, pattern), (guess_hbm, guess), (hamil_hbm, hamil)]
    pairs += [(filters_hbm, filters), (deriv_hbm, deriv), (atoms_hbm, atoms)]
    loads = [pltpu.make_async_copy(a, b, load_sems.at[i]) for i, (a, b) in enumerate(pairs)]
    for load in loads:
        load.start()
    for load in loads[:4]:
        load.wait()

    tall = pl.ds(pl.multiple_of(me.row * TALL, TALL), TALL)
    slim = pl.ds(pl.multiple_of(me.zl * SLIM, SLIM), SLIM)
    own_guess, own_ham = colp.at[0].at[tall, slim], hcol.at[tall, slim]
    kept = pattern[...].astype(F32)
    for i in range(TALL // BS):
        part = slice(i * BS, (i + 1) * BS)
        keep = mask_row(kept, i)
        here = me.row * TALL + i * BS + lax.broadcasted_iota(jnp.int32, (BS, SLIM), 0)
        there = me.col * SLIM + lax.broadcasted_iota(jnp.int32, (BS, SLIM), 1)
        half = jnp.where(here == there, 0.5, 0.0).astype(F32)
        own_guess[part] = ((half + guess[part].astype(F32)) * keep).astype(BF)
        own_ham[part] = jnp.where(keep > 0, hamil[part].astype(F32), 0.0).astype(BF)
    pl.semaphore_wait(barrier, len(peers))

    mine = pl.ds(pl.multiple_of((me.y * 4 + me.z) * ROWS, ROWS), ROWS)
    own_rows = pl.ds(pl.multiple_of(me.own * WIDE, WIDE), WIDE)
    chunk = [slice(c * CHUNK, (c + 1) * CHUNK) for c in range(CHUNKS)]
    row_sems = CHUNKS * ROW
    planes = 3 * row_sems
    plane_sems = [[planes], [planes + PLANE, planes + 2 * PLANE], [planes, planes + 3 * PLANE]]
    ham_sems = [planes + 4 * PLANE, planes + 5 * PLANE]
    filters_sem, energy_sem = planes + 6 * PLANE, planes + 6 * PLANE + 1

    def row_chunks(buf, send, group):
        return [Row(cp, me, buf, send, group * row_sems + c * ROW, c * CHUNK) for c in range(CHUNKS)]

    def drain_rows(buf, send):
        cp.sent(buf.at[:, : 7 * WIDE], send)

    cp.send(filters, others, 6, filters_sem, me.partner())
    panel = colp.at[0]
    plane = Plane(cp, me, panel, tall_piece(panel, 0, TALL // 2, 1), TALL // 2, SLIM, 2, plane_sems[0][0])
    whole = Row(cp, me, rowp, 0, 0, 0, ROWS)
    first = Product(rowp, panel)

    def whole_start():
        rowp[:, own_rows] = colp[0, mine]
        whole.start()

    def whole_shared():
        whole.shared_own()
        whole.shared()

    tasks = plane.tasks("A")
    tasks.update(R=whole_start, Ra=whole.arrive, Rs=whole_shared, E=lambda: first.blocks(me, EARLY))
    run(tasks, ORDER_A)
    plane.drain()
    cp.arrive(others, filters_sem)

    for step in range(2):
        drain_rows(rowp, 0)
        panel, after = colp.at[step], colp.at[1 - step]
        ham_piece = tall_piece(hcol, step * (TALL // 2), TALL // 4)
        ham = Plane(cp, me, hcol, ham_piece, TALL // 4, SLIM, 4 + step, ham_sems[step])
        pair = [
            Plane(cp, me, after, chunk_piece(after, 2 * i), CHUNK, WIDE, 3 - step, plane_sems[step + 1][i])
            for i in range(2)
        ]
        inner, rows, last = row_chunks(srow, 1, 1), row_chunks(rowp, 0, 0), row_chunks(grow, 7, 2)
        thirds = [Product(srow, panel, c * CHUNK, CHUNK) for c in range(CHUNKS)]
        own_piece, own_block = after.at[mine], rowp.at[:, own_rows]
        blocks = [filters[step].astype(F32), others[step].astype(F32)]
        keep = [jnp.where(me.zl == 0, m[:, :4], m[:, 4:]) for m in blocks]
        left = jnp.where(me.zl == 0, keep[0], keep[1])
        right = jnp.where(me.zl == 0, keep[1], keep[0])
        early = first.total
        upper, lower = Product(grow, after, 0, 3 * CHUNK), Product(grow, after, 3 * CHUNK, CHUNK)

        def square_chunk(c):
            tail = Product(rowp, panel, c * CHUNK, CHUNK)
            tail.total = early[chunk[c]]
            tail.blocks(me, LATE)
            srow[chunk[c], own_rows] = tail.total.astype(BF)
            inner[c].start()
            square[chunk[c]] = tail.total

        def third_chunk(c):
            inner[c].arrive()
            thirds[c].tiles(me, 0, 0, 1, 3, 2)

        def dens_chunk(c):
            inner[c].shared_own()
            inner[c].shared()
            thirds[c].tiles(me, 1, 0, 1, 3, 2)
            mask = jnp.concatenate([mask_row(left, c), mask_row(right, c)], axis=1)
            dens = (mask * (3.0 * square[chunk[c]] - 2.0 * thirds[c].total)).astype(BF)
            own_piece[chunk[c]] = dens
            own_block[chunk[c]] = dens

        def rows_start(c):
            if c == CHUNKS - 1:
                drain_rows(srow, 1)
            rows[c].start()

        def rows_shared(c):
            rows[c].shared_own()
            rows[c].shared()

        def inward(c):
            part = Product(rowp, hcol, c * CHUNK, CHUNK)
            part.tiles(me, 0, 0, 1, 3, 2)
            part.tiles(me, 1, 0, 1, 3, 2)
            grow[chunk[c], own_rows] = part.total.astype(BF)
            last[c].start()

        def last_shared(c):
            last[c].shared_own()
            last[c].shared()

        def give(c):
            for dk in range(2):
                k = (me.k + dk) % 2
                src = etile.at[pl.ds(pl.multiple_of(c * CHUNK + k * OWN, OWN), OWN)]
                target = me.by(dx=4 - me.x + c, dk=dk)

                def send():
                    cp.send(src, eall.at[:, own_rows], 8, energy_sem, target)

                if dk:
                    send()
                else:
                    pl.when(me.x != c)(send)

        def energy_upper():
            for dk in range(2):
                upper.tiles(me, dk, 0, 1, 3, 2)
            etile[: 3 * CHUNK] = upper.total.astype(BF)
            for c in range(3):
                give(c)

        def energy_lower():
            for dk in range(2):
                lower.tiles(me, dk, 0, 1, 3, 2)
            etile[3 * CHUNK :] = lower.total.astype(BF)
            give(3)

        tasks = {**ham.tasks("H"), **pair[0].tasks("P"), **pair[1].tasks("Q")}
        steps = dict(S=square_chunk, T=third_chunk, D=dens_chunk, R=rows_start, Rs=rows_shared, G=inward, Ls=last_shared)
        for c in range(CHUNKS):
            tasks.update({name + str(c): functools.partial(f, c) for name, f in steps.items()})
            tasks.update({"Ra" + str(c): rows[c].arrive, "La" + str(c): last[c].arrive})
        if step == 0:
            first = Product(rowp, after)
            tasks.update(E=functools.partial(first.blocks, me, EARLY))
        tasks.update(U=energy_upper, V=energy_lower)
        run(tasks, ORDER_B if step == 0 else ORDER_C)
        cp.sent(after.at[: 60 * CHUNK], 3 - step)
        ham.drain()

    drain_rows(rowp, 0)
    drain_rows(grow, 7)
    eall[:, own_rows] = etile[pl.ds(pl.multiple_of(me.own * OWN, OWN), OWN)]
    same = lax.broadcasted_iota(jnp.int32, (OWN, OWN), 0) == lax.broadcasted_iota(jnp.int32, (OWN, OWN), 1)
    loads[4].wait()
    loads[5].wait()
    atom_of = jnp.sum(jnp.where(same, atoms[...].astype(F32), 0.0), axis=1, keepdims=True)
    cp.sent(filters, 6)
    cp.arrive(eall.at[:, : 7 * WIDE], energy_sem)
    for b in range(8):
        for zl in range(2):
            energy_out[:, (zl * 8 + b) * SLIM : (zl * 8 + b + 1) * SLIM] = eall[
                :, b * WIDE + zl * SLIM : b * WIDE + (zl + 1) * SLIM
            ]
    wide = energy_out[...].astype(F32)
    line = lax.broadcasted_iota(jnp.int32, (3, ATOM_DEV), 0)
    lane = lax.broadcasted_iota(jnp.int32, (3, ATOM_DEV), 1)
    forces = jnp.zeros((3, ATOM_DEV), F32)
    for axis in range(3):
        per_row = jnp.sum(deriv[axis].astype(F32) * wide, axis=1, keepdims=True)
        for atom in range(ATOM_DEV):
            force = jnp.sum(jnp.where(atom_of == atom, per_row, 0.0))
            forces = jnp.where((line == axis) & (lane == atom), force, forces)
    forces_out[...] = forces
    cp.sent(eall.at[:, : 7 * WIDE], 8)


def body(hamil, guess, pattern, filters, deriv, atom_of_row):
    args = (hamil, guess, pattern.T, filters.transpose(0, 2, 1), deriv, atom_of_row.reshape(1, OWN))
    vmem = pl.BlockSpec(memory_space=pltpu.VMEM)
    return pl.pallas_call(
        kernel,
        out_shape=(
            jax.ShapeDtypeStruct((OWN, N), BF),
            jax.ShapeDtypeStruct((3, ATOM_DEV), F32),
        ),
        in_specs=[pl.BlockSpec(memory_space=pl.ANY)] * 6,
        out_specs=(vmem, vmem),
        scratch_shapes=[pltpu.VMEM(arg.shape, arg.dtype) for arg in args]
        + [
            pltpu.VMEM((ROWS, N), BF),
            pltpu.VMEM((2, N, WIDE), BF),
            pltpu.VMEM((ROWS, N), BF),
            pltpu.VMEM((ROWS, N), BF),
            pltpu.VMEM((N, WIDE), BF),
            pltpu.VMEM((ROWS, WIDE), F32),
            pltpu.VMEM((ROWS, WIDE), BF),
            pltpu.VMEM((OWN, N), BF),
            pltpu.VMEM(args[3].shape, args[3].dtype),
            pltpu.SemaphoreType.DMA((6,)),
            pltpu.SemaphoreType.DMA((9,)),
            pltpu.SemaphoreType.DMA((3 * CHUNKS * ROW + 6 * PLANE + 2,)),
        ],
        compiler_params=pltpu.CompilerParams(
            collective_id=0, has_side_effects=True, vmem_limit_bytes=60 * 1024 * 1024
        ),
    )(*args)


def solution(mesh):
    return jax.shard_map(
        body,
        mesh=mesh,
        in_specs=(
            P("row", "col"),
            P("row", "col"),
            P("row", "col"),
            P(None, "row", "col"),
            P(None, ("row", "col"), None),
            P(("row", "col")),
        ),
        out_specs=(P(("row", "col"), None), P(None, ("row", "col"))),
        check_vma=False,
    )
```

```python
import functools

import jax
import jax.numpy as jnp
from jax import lax
from jax.experimental import pallas as pl
from jax.experimental.pallas import tpu as pltpu
from jax.sharding import PartitionSpec as P

MESH = pl.DeviceIdType.MESH
BF, F32 = jnp.bfloat16, jnp.float32
BS = 64
ATOM_DEV = 4
N, OWN = 4096, 32
TALL, SLIM = 512, 256
ROWS, WIDE = 256, 512
SIZES = [[64, 64, 64, 64], [64, 64, 64, 64]]
PLANE, ROW = 16, 3


class Place:
    def __init__(self):
        row, col = lax.axis_index("row"), lax.axis_index("col")
        self.row, self.col = row, col
        self.zl = col // 8
        self.x, self.y, self.z, self.k = (col // 2) % 4, row // 2, (row % 2) * 2 + col // 8, col % 2
        self.own = self.x * 2 + self.k

    def at(self, x, y, z, k):
        return (y * 2 + z // 2, (z % 2) * 8 + x * 2 + k)

    def by(self, dx=0, dy=0, dz=0, dk=0):
        return self.at((self.x + dx) % 4, (self.y + dy) % 4, (self.z + dz) % 4, (self.k + dk) % 2)

    def partner(self):
        return (self.row, (self.col + 8) % 16)

    def line(self, dx, dk=0):
        return (self.x + dx) % 4 * 2 + (self.k + dk) % 2


class Copies:
    def __init__(self, me, send_sems, recv_sems):
        self.send_sems, self.recv_sems, self.any = send_sems, recv_sems, me.by(dx=1)

    def make(self, src, dst, send, recv, device):
        return pltpu.make_async_remote_copy(
            src_ref=src,
            dst_ref=dst,
            send_sem=self.send_sems.at[send],
            recv_sem=self.recv_sems.at[recv],
            device_id=device,
            device_id_type=MESH,
        )

    def send(self, src, dst, send, recv, device):
        self.make(src, dst, send, recv, device).start()

    def arrive(self, ref, recv):
        self.make(ref, ref, 0, recv, self.any).wait_recv()

    def sent(self, ref, send):
        self.make(ref, ref, send, 0, self.any).wait_send()


def chunk_piece(buf, first, rows):
    def piece(y, z, t, lo, size):
        start = (y * 4 + z) * ROWS + first + t * rows + lo
        return buf.at[pl.ds(pl.multiple_of(start, 16), size)]

    return piece


def tall_piece(buf, first, rows, swap=0):
    def piece(y, z, t, lo, size):
        start = (y * 2 + z // 2) * TALL + first + (t + swap * z) % 2 * rows + lo
        return buf.at[
            pl.ds(pl.multiple_of(start, 64), size), pl.ds(pl.multiple_of(z % 2 * SLIM, SLIM), SLIM)
        ]

    return piece


class Plane:
    def __init__(self, cp, me, buf, piece, rows, width, send, recv):
        self.cp, self.me, self.buf, self.piece = cp, me, buf, piece
        self.rows, self.send, self.recv = rows, send, recv
        self.equal = rows * width // WIDE

    def ref(self, t, i, j, lo=0, size=None):
        back = (i, j) if t == 0 else (j, i)
        y, z = (self.me.y + 4 - back[0]) % 4, (self.me.z + 4 - back[1]) % 4
        return self.piece(y, z, t, lo, self.rows if size is None else size)

    def put(self, t, i, j, axis, d, sem, lo=0, size=None):
        ref = self.ref(t, i, j, lo, size)
        device = self.me.by(dy=d) if axis == t else self.me.by(dz=d)
        self.cp.send(ref, ref, self.send, self.recv + sem, device)

    def got(self, sem, pieces=1):
        self.cp.arrive(self.buf.at[: pieces * self.equal], self.recv + sem)

    def own_first(self, t):
        self.put(t, 0, 0, 0, 1, 7 * t)
        self.put(t, 0, 0, 0, 3, 7 * t + 1)

    def own_second(self, t):
        self.put(t, 0, 0, 1, 1, 7 * t + 3)
        self.put(t, 0, 0, 1, 3, 7 * t + 3)

    def ring(self, t):
        half = self.rows // 2
        self.got(7 * t)
        self.put(t, 1, 0, 0, 1, 7 * t + 2, 0, half)
        self.got(7 * t + 1)
        self.put(t, 3, 0, 0, 3, 7 * t + 2, half, half)

    def spread(self, t):
        self.put(t, 1, 0, 1, 3, 7 * t + 4)
        self.put(t, 3, 0, 1, 1, 7 * t + 5)
        self.put(t, 1, 0, 1, 1, 14)
        self.put(t, 3, 0, 1, 3, 14)

    def own_far(self, t):
        self.got(7 * t + 3, 2)
        self.put(t, 0, 1, 1, 1, 15)

    def spread_far(self, t):
        self.got(7 * t + 2)
        self.put(t, 2, 0, 1, 3, 7 * t + 6)
        self.put(t, 2, 0, 1, 1, 14)

    def left_far(self, t):
        self.got(7 * t + 4)
        self.put(t, 1, 3, 1, 3, 15)

    def right_far(self, t):
        self.got(7 * t + 5)
        self.put(t, 3, 1, 1, 1, 15)

    def far_far(self, t):
        self.got(7 * t + 6)
        self.put(t, 2, 3, 1, 3, 15)

    def tasks(self, name):
        steps = [self.own_first, self.own_second, self.ring, self.spread, self.own_far]
        steps += [self.spread_far, self.left_far, self.right_far, self.far_far]
        out = {name + str(t) + l: functools.partial(f, t) for l, f in zip("abcdefghi", steps) for t in range(2)}
        return {**out, name + "n": self.near, name + "z": self.far}

    def near(self):
        self.got(14, 6)

    def far(self):
        self.got(15, 8)

    def drain(self):
        self.cp.sent(self.buf.at[: 30 * self.equal], self.send)


class Row:
    def __init__(self, cp, me, buf, send, recv, lo, size):
        self.cp, self.me, self.buf, self.send, self.recv = cp, me, buf, send, recv
        self.lo, self.size = lo, size

    def put(self, d, to, sem, dk=0):
        at = pl.multiple_of(self.me.line(4 - d) * WIDE, WIDE)
        ref = self.buf.at[self.lo : self.lo + self.size, pl.ds(at, WIDE)]
        self.cp.send(ref, ref, self.send, self.recv + sem, self.me.by(dx=to, dk=dk))

    def got(self, sem, tiles=1):
        self.cp.arrive(self.buf.at[: self.size, : tiles * WIDE], self.recv + sem)

    def start(self):
        self.put(0, 1, 0)
        self.put(0, 3, 0)
        self.put(0, 2, 1)
        self.put(0, 0, 2, dk=1)

    def arrive(self):
        self.got(0, 2)
        self.put(1, 0, 2, dk=1)
        self.put(3, 0, 2, dk=1)
        self.got(1)
        self.put(2, 0, 2, dk=1)

    def shared(self):
        self.got(2, 4)


def dot(a, b):
    return jnp.dot(a, b, preferred_element_type=F32)


def block_k(b, zl):
    return pl.ds(pl.multiple_of((zl * 8 + b) * ROWS, ROWS), ROWS)


class Product:
    def __init__(self, left, right, lo=0, size=ROWS):
        self.left, self.right, self.rows, self.total = left, right, slice(lo, lo + size), None

    def add(self, b, zl):
        at = pl.ds(pl.multiple_of(b * WIDE + zl * SLIM, SLIM), SLIM)
        term = dot(self.left[self.rows, at], self.right[block_k(b, zl)])
        self.total = term if self.total is None else self.total + term

    def tiles(self, me, dk, *ds):
        for d in ds:
            for zl in range(2):
                self.add(me.line(4 - d, dk), zl)

    def blocks(self, me, pairs):
        for dy, dz in pairs:
            r = (me.y + 4 - dy) % 4 * 4 + (me.z + 4 - dz) % 4
            self.add(r % 8, r // 8)


EARLY = [(dy, dz) for dy in (0, 1, 3) for dz in (0, 1, 3)]
LATE = [(d, 2) for d in range(4)] + [(2, d) for d in (0, 1, 3)]


def mask_row(blocks, i):
    count = blocks.shape[0]
    lane = lax.broadcasted_iota(jnp.int32, (1, count * BS), 1) // BS
    row = jnp.zeros((1, count * BS), F32)
    for j in range(count):
        row = jnp.where(lane == j, blocks[j : j + 1, i : i + 1], row)
    return row


def run(tasks, order):
    for name in order:
        tasks[name]()


ORDER_A = [
    "A0a", "A1a", "A0b", "A1b", "A0c", "A1c", "R", "A1d", "A0d", "A1f", "A0f", "A1h", "A1g", "A0h", "A0g", "A1e",
    "A1i", "A0e", "A0i", "H1a", "H0a", "H1b", "Ra", "Rs", "An", "H0b", "E", "Az",
]
ORDER_B = [
    "S0", "S1", "H1c", "H0c", "H1d", "H0d", "S2", "S3", "H0e", "H1e", "H0f", "H1f", "H1g", "T0", "H0h", "H0g", "D0",
    "P0b", "P0a", "H1h", "T1", "H0i", "H1i", "D1", "P1a", "P1b", "T2", "P0c", "R0", "P0d", "R1", "D2", "Q0a", "T3",
    "P1c", "P1d", "D3", "Q1a", "R3", "Q0c", "Q0d", "Hn", "Q1b", "P1f", "Q1c", "P0f", "P1e", "Ra0", "Q1d", "Q0b",
    "Q0f", "P0e", "Q1e", "P1g", "R2", "Q1f", "Q0h", "P1i", "P0g", "P1h", "P0h", "P0i", "Q1h", "Q1g", "Q0g", "Ra3",
    "Rs3", "Q0i", "Hz", "Ra1", "Q0e", "Q1i", "Ra2", "Pn", "I0a", "Rs0", "Qn", "I1a", "Rs2", "Rs1", "Pz", "E", "I0b",
    "Qz",
]
ORDER_C = [
    "S0", "S1", "I1b", "I1c", "I0c", "I0d", "S2", "I1d", "S3", "I0f", "I1f", "T0", "I1g", "I0g", "I1e", "D0", "T1",
    "I0i", "I0h", "I0e", "P0a", "D1", "R1", "T2", "I1h", "P1a", "R0", "P0b", "I1i", "D2", "Q0a", "Q0b", "T3", "P1b",
    "R2", "In", "D3", "Q1b", "Q1a", "Iz", "P1c", "P0c", "Q0c", "Ra1", "P1d", "P0e", "Q0d", "R3", "P1e", "Ra0",
    "Q1c", "Rs1", "G1", "Q1d", "P1f", "P0f", "P0d", "Rs0", "G0", "Ra2", "Ra3", "Q0f", "Rs2", "Q1f", "G2", "Q1e",
    "P0i", "Rs3", "Q1g", "G3", "Q0g", "Q0h", "P1i", "La1", "P1h", "P0g", "Q0e", "Q1i", "Pn", "La0", "Ls1", "P1g",
    "Q1h", "Q0i", "P0h", "La2", "Pz", "Qn", "Qz", "Ls2", "Ls0", "La3", "U", "Ls3", "V",
]


def kernel(
    hamil_hbm, guess_hbm, pattern_hbm, filters_hbm, deriv_hbm, atoms_hbm,
    energy_out, forces_out,
    hamil, guess, pattern, filters, deriv, atoms,
    rowp, colp, srow, grow, hcol, square, etile, eall, others, load_sems, send_sems, recv_sems,
):
    me = Place()
    cp = Copies(me, send_sems, recv_sems)
    peers = [me.by(dx=dx, dk=dk) for dx in range(4) for dk in range(2)][1:]
    peers += [me.by(dy=1), me.by(dy=3), me.by(dz=1), me.by(dz=3)]
    barrier = pltpu.get_barrier_semaphore()
    for peer in peers:
        pl.semaphore_signal(barrier, inc=1, device_id=peer, device_id_type=MESH)

    pairs = [(pattern_hbm, pattern), (guess_hbm, guess), (hamil_hbm, hamil)]
    pairs += [(filters_hbm, filters), (deriv_hbm, deriv), (atoms_hbm, atoms)]
    loads = [pltpu.make_async_copy(a, b, load_sems.at[i]) for i, (a, b) in enumerate(pairs)]
    for load in loads:
        load.start()
    for load in loads[:4]:
        load.wait()

    tall = pl.ds(pl.multiple_of(me.row * TALL, TALL), TALL)
    slim = pl.ds(pl.multiple_of(me.zl * SLIM, SLIM), SLIM)
    own_guess, own_ham = colp.at[0].at[tall, slim], hcol.at[tall, slim]
    kept = pattern[...].astype(F32)
    for i in range(TALL // BS):
        part = slice(i * BS, (i + 1) * BS)
        keep = mask_row(kept, i)
        here = me.row * TALL + i * BS + lax.broadcasted_iota(jnp.int32, (BS, SLIM), 0)
        there = me.col * SLIM + lax.broadcasted_iota(jnp.int32, (BS, SLIM), 1)
        half = jnp.where(here == there, 0.5, 0.0).astype(F32)
        own_guess[part] = ((half + guess[part].astype(F32)) * keep).astype(BF)
        own_ham[part] = jnp.where(keep > 0, hamil[part].astype(F32), 0.0).astype(BF)
    pl.semaphore_wait(barrier, len(peers))

    mine = pl.ds(pl.multiple_of((me.y * 4 + me.z) * ROWS, ROWS), ROWS)
    own_rows = pl.ds(pl.multiple_of(me.own * WIDE, WIDE), WIDE)
    row_sems = max(map(len, SIZES)) * ROW
    planes = 3 * row_sems
    odd_sems = [planes + i * PLANE for i in range(len(SIZES[0]) // 2)]
    even_sems = [planes + (len(odd_sems) + i) * PLANE for i in range(len(SIZES[1]) // 2)]
    ham_first = planes + (len(odd_sems) + len(even_sems)) * PLANE
    ham_sems = [ham_first, ham_first + PLANE]
    filters_sem, energy_sem = ham_first + 2 * PLANE, ham_first + 2 * PLANE + 1

    def row_chunks(buf, send, group, sizes):
        return [
            Row(cp, me, buf, send, group * row_sems + c * ROW, sum(sizes[:c]), size) for c, size in enumerate(sizes)
        ]

    def drain_rows(buf, send):
        cp.sent(buf.at[:, : 7 * WIDE], send)

    hams = []
    for i in range(2):
        piece = tall_piece(hcol, i * (TALL // 2), TALL // 4)
        hams.append(Plane(cp, me, hcol, piece, TALL // 4, SLIM, 4 + i, ham_sems[i]))
    ham_tasks = {**hams[0].tasks("H"), **hams[1].tasks("I")}

    cp.send(filters, others, 6, filters_sem, me.partner())
    panel = colp.at[0]
    plane = Plane(cp, me, panel, tall_piece(panel, 0, TALL // 2, 1), TALL // 2, SLIM, 2, even_sems[0])
    whole = Row(cp, me, rowp, 0, 0, 0, ROWS)
    first = Product(rowp, panel)

    def whole_start():
        rowp[:, own_rows] = colp[0, mine]
        whole.start()

    tasks = {**plane.tasks("A"), **ham_tasks}
    tasks.update(R=whole_start, Ra=whole.arrive, Rs=whole.shared, E=lambda: first.blocks(me, EARLY))
    run(tasks, ORDER_A)
    plane.drain()
    cp.arrive(others, filters_sem)

    for step in range(2):
        drain_rows(rowp, 0)
        panel, after = colp.at[step], colp.at[1 - step]
        sizes = SIZES[step]
        count = len(sizes)
        chunk = [slice(sum(sizes[:c]), sum(sizes[: c + 1])) for c in range(count)]
        sems = odd_sems if step == 0 else even_sems
        pairs = []
        for i in range(0, count, 2):
            piece = chunk_piece(after, chunk[i].start, sizes[i])
            pairs.append(Plane(cp, me, after, piece, sizes[i], WIDE, 3 - step, sems[i // 2]))
        inner, rows = row_chunks(srow, 1, 1, sizes), row_chunks(rowp, 0, 0, sizes)
        last = row_chunks(grow, 7, 2, sizes)
        thirds = [Product(srow, panel, chunk[c].start, sizes[c]) for c in range(count)]
        own_piece, own_block = after.at[mine], rowp.at[:, own_rows]
        blocks = [filters[step].astype(F32), others[step].astype(F32)]
        keep = [jnp.where(me.zl == 0, m[:, :4], m[:, 4:]) for m in blocks]
        left = jnp.where(me.zl == 0, keep[0], keep[1])
        right = jnp.where(me.zl == 0, keep[1], keep[0])
        early = first.total
        cut = chunk[-1].start
        upper, lower = Product(grow, after, 0, cut), Product(grow, after, cut, sizes[-1])

        def square_chunk(c):
            tail = Product(rowp, panel, chunk[c].start, sizes[c])
            tail.total = early[chunk[c]]
            tail.blocks(me, LATE)
            srow[chunk[c], own_rows] = tail.total.astype(BF)
            inner[c].start()
            square[chunk[c]] = tail.total

        def third_chunk(c):
            inner[c].arrive()
            thirds[c].tiles(me, 0, 0, 1, 3, 2)

        def dens_chunk(c):
            inner[c].shared()
            thirds[c].tiles(me, 1, 0, 1, 3, 2)
            lo = chunk[c].start
            while lo < chunk[c].stop:
                hi = min(lo // BS * BS + BS, chunk[c].stop)
                mask = jnp.concatenate([mask_row(left, lo // BS), mask_row(right, lo // BS)], axis=1)
                third = thirds[c].total[lo - chunk[c].start : hi - chunk[c].start]
                dens = (mask * (3.0 * square[lo:hi] - 2.0 * third)).astype(BF)
                own_piece[lo:hi] = dens
                own_block[lo:hi] = dens
                lo = hi

        def rows_start(c):
            if c == count - 1:
                drain_rows(srow, 1)
            rows[c].start()

        def inward(c):
            part = Product(rowp, hcol, chunk[c].start, sizes[c])
            part.tiles(me, 0, 0, 1, 3, 2)
            part.tiles(me, 1, 0, 1, 3, 2)
            grow[chunk[c], own_rows] = part.total.astype(BF)
            last[c].start()

        def give(lo, hi):
            for owner in range(lo // OWN, hi // OWN):
                src = etile.at[owner * OWN : (owner + 1) * OWN]
                target = me.at(owner // 2, me.y, me.z, owner % 2)

                @pl.when(me.own != owner)
                def _():
                    cp.send(src, eall.at[:, own_rows], 8, energy_sem, target)

        def energy_upper():
            for dk in range(2):
                upper.tiles(me, dk, 0, 1, 3, 2)
            etile[:cut] = upper.total.astype(BF)
            give(0, cut)

        def energy_lower():
            for dk in range(2):
                lower.tiles(me, dk, 0, 1, 3, 2)
            etile[cut:] = lower.total.astype(BF)
            give(cut, ROWS)

        tasks = dict(ham_tasks)
        for name, pair in zip("PQW", pairs):
            tasks.update(pair.tasks(name))
        steps = dict(S=square_chunk, T=third_chunk, D=dens_chunk, R=rows_start, G=inward)
        for c in range(count):
            tasks.update({name + str(c): functools.partial(f, c) for name, f in steps.items()})
            tasks.update({"Ra" + str(c): rows[c].arrive, "Rs" + str(c): rows[c].shared})
            tasks.update({"La" + str(c): last[c].arrive, "Ls" + str(c): last[c].shared})
        if step == 0:
            first = Product(rowp, after)
            tasks.update(E=functools.partial(first.blocks, me, EARLY))
        tasks.update(U=energy_upper, V=energy_lower)
        run(tasks, ORDER_B if step == 0 else ORDER_C)
        cp.sent(after.at[: 15 * ROWS], 3 - step)

    for ham in hams:
        ham.drain()
    drain_rows(rowp, 0)
    drain_rows(grow, 7)
    eall[:, own_rows] = etile[pl.ds(pl.multiple_of(me.own * OWN, OWN), OWN)]
    same = lax.broadcasted_iota(jnp.int32, (OWN, OWN), 0) == lax.broadcasted_iota(jnp.int32, (OWN, OWN), 1)
    loads[4].wait()
    loads[5].wait()
    atom_of = jnp.sum(jnp.where(same, atoms[...].astype(F32), 0.0), axis=1, keepdims=True)
    cp.sent(filters, 6)
    cp.arrive(eall.at[:, : 7 * WIDE], energy_sem)
    for b in range(8):
        for zl in range(2):
            energy_out[:, (zl * 8 + b) * SLIM : (zl * 8 + b + 1) * SLIM] = eall[
                :, b * WIDE + zl * SLIM : b * WIDE + (zl + 1) * SLIM
            ]
    wide = energy_out[...].astype(F32)
    line = lax.broadcasted_iota(jnp.int32, (3, ATOM_DEV), 0)
    lane = lax.broadcasted_iota(jnp.int32, (3, ATOM_DEV), 1)
    forces = jnp.zeros((3, ATOM_DEV), F32)
    for axis in range(3):
        per_row = jnp.sum(deriv[axis].astype(F32) * wide, axis=1, keepdims=True)
        for atom in range(ATOM_DEV):
            force = jnp.sum(jnp.where(atom_of == atom, per_row, 0.0))
            forces = jnp.where((line == axis) & (lane == atom), force, forces)
    forces_out[...] = forces
    cp.sent(eall.at[:, : 7 * WIDE], 8)


def body(hamil, guess, pattern, filters, deriv, atom_of_row):
    args = (hamil, guess, pattern.T, filters.transpose(0, 2, 1), deriv, atom_of_row.reshape(1, OWN))
    vmem = pl.BlockSpec(memory_space=pltpu.VMEM)
    sems = 3 * max(map(len, SIZES)) * ROW + (sum(map(len, SIZES)) // 2 + 2) * PLANE + 2
    return pl.pallas_call(
        kernel,
        out_shape=(
            jax.ShapeDtypeStruct((OWN, N), BF),
            jax.ShapeDtypeStruct((3, ATOM_DEV), F32),
        ),
        in_specs=[pl.BlockSpec(memory_space=pl.ANY)] * 6,
        out_specs=(vmem, vmem),
        scratch_shapes=[pltpu.VMEM(arg.shape, arg.dtype) for arg in args]
        + [
            pltpu.VMEM((ROWS, N), BF),
            pltpu.VMEM((2, N, WIDE), BF),
            pltpu.VMEM((ROWS, N), BF),
            pltpu.VMEM((ROWS, N), BF),
            pltpu.VMEM((N, WIDE), BF),
            pltpu.VMEM((ROWS, WIDE), F32),
            pltpu.VMEM((ROWS, WIDE), BF),
            pltpu.VMEM((OWN, N), BF),
            pltpu.VMEM(args[3].shape, args[3].dtype),
            pltpu.SemaphoreType.DMA((6,)),
            pltpu.SemaphoreType.DMA((9,)),
            pltpu.SemaphoreType.DMA((sems,)),
        ],
        compiler_params=pltpu.CompilerParams(
            collective_id=0, has_side_effects=True, vmem_limit_bytes=60 * 1024 * 1024
        ),
    )(*args)


def solution(mesh):
    return jax.shard_map(
        body,
        mesh=mesh,
        in_specs=(
            P("row", "col"),
            P("row", "col"),
            P("row", "col"),
            P(None, "row", "col"),
            P(None, ("row", "col"), None),
            P(("row", "col")),
        ),
        out_specs=(P(("row", "col"), None), P(None, ("row", "col"))),
        check_vma=False,
    )
```

```python
import functools

import jax
import jax.numpy as jnp
from jax import lax
from jax.experimental import pallas as pl
from jax.experimental.pallas import tpu as pltpu
from jax.sharding import PartitionSpec as P

MESH = pl.DeviceIdType.MESH
BF, F32 = jnp.bfloat16, jnp.float32
BS = 64
ATOM_DEV = 4
N, OWN = 4096, 32
TALL, SLIM = 512, 256
ROWS, WIDE = 256, 512
SIZES = [[64, 64, 64, 64], [64, 64, 64, 64]]
PLANE, ROW = 16, 3


class Place:
    def __init__(self):
        row, col = lax.axis_index("row"), lax.axis_index("col")
        self.row, self.col = row, col
        self.zl = col // 8
        self.x, self.y, self.z, self.k = (col // 2) % 4, row // 2, (row % 2) * 2 + col // 8, col % 2
        self.own = self.x * 2 + self.k

    def at(self, x, y, z, k):
        return (y * 2 + z // 2, (z % 2) * 8 + x * 2 + k)

    def by(self, dx=0, dy=0, dz=0, dk=0):
        return self.at((self.x + dx) % 4, (self.y + dy) % 4, (self.z + dz) % 4, (self.k + dk) % 2)

    def partner(self):
        return (self.row, (self.col + 8) % 16)

    def line(self, dx, dk=0):
        return (self.x + dx) % 4 * 2 + (self.k + dk) % 2


class Copies:
    def __init__(self, me, send_sems, recv_sems):
        self.send_sems, self.recv_sems, self.any = send_sems, recv_sems, me.by(dx=1)

    def make(self, src, dst, send, recv, device):
        return pltpu.make_async_remote_copy(
            src_ref=src,
            dst_ref=dst,
            send_sem=self.send_sems.at[send],
            recv_sem=self.recv_sems.at[recv],
            device_id=device,
            device_id_type=MESH,
        )

    def send(self, src, dst, send, recv, device):
        self.make(src, dst, send, recv, device).start()

    def arrive(self, ref, recv):
        self.make(ref, ref, 0, recv, self.any).wait_recv()

    def sent(self, ref, send):
        self.make(ref, ref, send, 0, self.any).wait_send()


def chunk_piece(buf, first, rows):
    def piece(y, z, t, lo, size):
        start = (y * 4 + z) * ROWS + first + t * rows + lo
        return buf.at[pl.ds(pl.multiple_of(start, 16), size)]

    return piece


def tall_piece(buf, first, rows, swap=0):
    def piece(y, z, t, lo, size):
        start = (y * 2 + z // 2) * TALL + first + (t + swap * z) % 2 * rows + lo
        return buf.at[
            pl.ds(pl.multiple_of(start, 64), size), pl.ds(pl.multiple_of(z % 2 * SLIM, SLIM), SLIM)
        ]

    return piece


class Plane:
    def __init__(self, cp, me, buf, piece, rows, width, send, recv):
        self.cp, self.me, self.buf, self.piece = cp, me, buf, piece
        self.rows, self.send, self.recv = rows, send, recv
        self.equal = rows * width // WIDE

    def ref(self, t, i, j, lo=0, size=None):
        back = (i, j) if t == 0 else (j, i)
        y, z = (self.me.y + 4 - back[0]) % 4, (self.me.z + 4 - back[1]) % 4
        return self.piece(y, z, t, lo, self.rows if size is None else size)

    def put(self, t, i, j, axis, d, sem, lo=0, size=None):
        ref = self.ref(t, i, j, lo, size)
        device = self.me.by(dy=d) if axis == t else self.me.by(dz=d)
        self.cp.send(ref, ref, self.send, self.recv + sem, device)

    def got(self, sem, pieces=1):
        self.cp.arrive(self.buf.at[: pieces * self.equal], self.recv + sem)

    def own_first(self, t):
        self.put(t, 0, 0, 0, 1, 7 * t)
        self.put(t, 0, 0, 0, 3, 7 * t + 1)

    def own_second(self, t):
        self.put(t, 0, 0, 1, 1, 7 * t + 3)
        self.put(t, 0, 0, 1, 3, 7 * t + 3)

    def ring(self, t):
        half = self.rows // 2
        self.got(7 * t)
        self.put(t, 1, 0, 0, 1, 7 * t + 2, 0, half)
        self.got(7 * t + 1)
        self.put(t, 3, 0, 0, 3, 7 * t + 2, half, half)

    def spread(self, t):
        self.put(t, 1, 0, 1, 3, 7 * t + 4)
        self.put(t, 3, 0, 1, 1, 7 * t + 5)
        self.put(t, 1, 0, 1, 1, 14)
        self.put(t, 3, 0, 1, 3, 14)

    def own_far(self, t):
        self.got(7 * t + 3, 2)
        self.put(t, 0, 1, 1, 1, 15)

    def spread_far(self, t):
        self.got(7 * t + 2)
        self.put(t, 2, 0, 1, 3, 7 * t + 6)
        self.put(t, 2, 0, 1, 1, 14)

    def left_far(self, t):
        self.got(7 * t + 4)
        self.put(t, 1, 3, 1, 3, 15)

    def right_far(self, t):
        self.got(7 * t + 5)
        self.put(t, 3, 1, 1, 1, 15)

    def far_far(self, t):
        self.got(7 * t + 6)
        self.put(t, 2, 3, 1, 3, 15)

    def tasks(self, name):
        steps = [self.own_first, self.own_second, self.ring, self.spread, self.own_far]
        steps += [self.spread_far, self.left_far, self.right_far, self.far_far]
        out = {name + str(t) + l: functools.partial(f, t) for l, f in zip("abcdefghi", steps) for t in range(2)}
        return {**out, name + "n": self.near, name + "z": self.far}

    def near(self):
        self.got(14, 6)

    def far(self):
        self.got(15, 8)

    def drain(self):
        self.cp.sent(self.buf.at[: 30 * self.equal], self.send)


class Row:
    def __init__(self, cp, me, buf, send, recv, lo, size):
        self.cp, self.me, self.buf, self.send, self.recv = cp, me, buf, send, recv
        self.lo, self.size = lo, size

    def put(self, d, to, sem, dk=0):
        at = pl.multiple_of(self.me.line(4 - d) * WIDE, WIDE)
        ref = self.buf.at[self.lo : self.lo + self.size, pl.ds(at, WIDE)]
        self.cp.send(ref, ref, self.send, self.recv + sem, self.me.by(dx=to, dk=dk))

    def got(self, sem, tiles=1):
        self.cp.arrive(self.buf.at[: self.size, : tiles * WIDE], self.recv + sem)

    def start(self):
        self.put(0, 1, 0)
        self.put(0, 3, 0)
        self.put(0, 2, 1)
        self.put(0, 0, 2, dk=1)

    def arrive(self):
        self.got(0, 2)
        self.put(1, 0, 2, dk=1)
        self.put(3, 0, 2, dk=1)
        self.got(1)
        self.put(2, 0, 2, dk=1)

    def shared(self):
        self.got(2, 4)


def dot(a, b):
    return jnp.dot(a, b, preferred_element_type=F32)


def block_k(b, zl):
    return pl.ds(pl.multiple_of((zl * 8 + b) * ROWS, ROWS), ROWS)


class Product:
    def __init__(self, left, right, lo=0, size=ROWS):
        self.left, self.right, self.rows, self.total = left, right, slice(lo, lo + size), None

    def add(self, b, zl):
        at = pl.ds(pl.multiple_of(b * WIDE + zl * SLIM, SLIM), SLIM)
        term = dot(self.left[self.rows, at], self.right[block_k(b, zl)])
        self.total = term if self.total is None else self.total + term

    def tiles(self, me, dk, *ds):
        for d in ds:
            for zl in range(2):
                self.add(me.line(4 - d, dk), zl)

    def blocks(self, me, pairs):
        for dy, dz in pairs:
            r = (me.y + 4 - dy) % 4 * 4 + (me.z + 4 - dz) % 4
            self.add(r % 8, r // 8)


EARLY = [(dy, dz) for dy in (0, 1, 3) for dz in (0, 1, 3)]
LATE = [(d, 2) for d in range(4)] + [(2, d) for d in (0, 1, 3)]


def mask_row(blocks, i):
    count = blocks.shape[0]
    lane = lax.broadcasted_iota(jnp.int32, (1, count * BS), 1) // BS
    row = jnp.zeros((1, count * BS), F32)
    for j in range(count):
        row = jnp.where(lane == j, blocks[j : j + 1, i : i + 1], row)
    return row


def run(tasks, order):
    for name in order:
        tasks[name]()


ORDER_A = [
    "A1a", "A0a", "A1b", "A0b", "A1c", "A0c", "A1d", "A0d", "R", "A0f", "A1f", "A0e", "A0h", "A1e", "A1h", "A0g",
    "A1g", "A0i", "A1i", "An", "H1a", "Ra", "H0a", "H0b", "Rs", "H1b", "E", "Az",
]
ORDER_B = [
    "S0", "H1c", "H0c", "H0d", "S1", "H1d", "S2", "S3", "H1f", "H1g", "T0", "H1h", "H0e", "H0g", "H0f", "D0", "P0a",
    "T1", "H1i", "H1e", "P0b", "D1", "P1a", "T2", "P1b", "P0c", "P0d", "D2", "Q0a", "Hn", "T3", "P1c", "P1d", "Q0b",
    "R0", "D3", "R3", "Q1a", "Q0c", "P0f", "Q1b", "H0h", "H0i", "P1f", "R1", "R2", "Q1c", "Q1d", "Q0f", "Q0d",
    "P0g", "Q0e", "P0h", "P1i", "P1e", "P0i", "Q1f", "P0e", "Ra0", "Ra1", "Q1h", "P1g", "Hz", "Q0h", "P1h", "Ra3",
    "Q0g", "Rs0", "Q1g", "Q0i", "I1a", "Q1e", "Pn", "Q1i", "Ra2", "Qn", "I0a", "Pz", "Rs3", "Rs1", "Rs2", "I0b",
    "I1b", "E", "Qz",
]
ORDER_C = [
    "S0", "I1c", "I0c", "I1d", "I0d", "S1", "I1f", "S2", "I0f", "T0", "I0e", "I1e", "I1g", "I0g", "S3", "I0h", "D0",
    "I1h", "P0a", "P0b", "T1", "I0i", "D1", "R1", "P1a", "I1i", "T2", "P1b", "R0", "D2", "Q0b", "Q0a", "R2", "T3",
    "P1c", "P1d", "P0c", "In", "D3", "Q1a", "P0d", "Q1b", "R3", "Ra1", "Q0c", "Rs1", "Iz", "G1", "Q1c", "P1h",
    "Ra0", "Q0d", "P1f", "Rs0", "Q1d", "G0", "Ra2", "P0f", "Q1f", "Q0f", "P0e", "Q0h", "Rs2", "Q0g", "Q1e", "P1g",
    "Ra3", "Q0e", "P0g", "P1e", "G2", "Q1g", "Q1h", "P0i", "P1i", "Rs3", "G3", "La1", "Q1i", "Q0i", "P0h", "La0",
    "Qn", "La2", "Ls1", "Ls0", "Pn", "Qz", "Pz", "Ls2", "U", "La3", "Ls3", "V",
]


def kernel(
    hamil_hbm, guess_hbm, pattern_hbm, filters_hbm, deriv_hbm, atoms_hbm,
    energy_out, forces_out,
    hamil, guess, pattern, filters, deriv, atoms,
    rowp, colp, srow, grow, hcol, square, etile, eall, others, load_sems, send_sems, recv_sems,
):
    me = Place()
    cp = Copies(me, send_sems, recv_sems)
    peers = [me.by(dx=dx, dk=dk) for dx in range(4) for dk in range(2)][1:]
    peers += [me.by(dy=1), me.by(dy=3), me.by(dz=1), me.by(dz=3)]
    barrier = pltpu.get_barrier_semaphore()
    for peer in peers:
        pl.semaphore_signal(barrier, inc=1, device_id=peer, device_id_type=MESH)

    pairs = [(pattern_hbm, pattern), (guess_hbm, guess), (hamil_hbm, hamil)]
    pairs += [(filters_hbm, filters), (deriv_hbm, deriv), (atoms_hbm, atoms)]
    loads = [pltpu.make_async_copy(a, b, load_sems.at[i]) for i, (a, b) in enumerate(pairs)]
    for load in loads:
        load.start()
    for load in loads[:4]:
        load.wait()

    tall = pl.ds(pl.multiple_of(me.row * TALL, TALL), TALL)
    slim = pl.ds(pl.multiple_of(me.zl * SLIM, SLIM), SLIM)
    own_guess, own_ham = colp.at[0].at[tall, slim], hcol.at[tall, slim]
    kept = pattern[...].astype(F32)
    for i in range(TALL // BS):
        part = slice(i * BS, (i + 1) * BS)
        keep = mask_row(kept, i)
        here = me.row * TALL + i * BS + lax.broadcasted_iota(jnp.int32, (BS, SLIM), 0)
        there = me.col * SLIM + lax.broadcasted_iota(jnp.int32, (BS, SLIM), 1)
        half = jnp.where(here == there, 0.5, 0.0).astype(F32)
        own_guess[part] = ((half + guess[part].astype(F32)) * keep).astype(BF)
        own_ham[part] = jnp.where(keep > 0, hamil[part].astype(F32), 0.0).astype(BF)
    pl.semaphore_wait(barrier, len(peers))

    mine = pl.ds(pl.multiple_of((me.y * 4 + me.z) * ROWS, ROWS), ROWS)
    own_rows = pl.ds(pl.multiple_of(me.own * WIDE, WIDE), WIDE)
    row_sems = max(map(len, SIZES)) * ROW
    planes = 3 * row_sems
    odd_sems = [planes + i * PLANE for i in range(len(SIZES[0]) // 2)]
    even_sems = [planes + (len(odd_sems) + i) * PLANE for i in range(len(SIZES[1]) // 2)]
    ham_first = planes + (len(odd_sems) + len(even_sems)) * PLANE
    ham_sems = [ham_first, ham_first + PLANE]
    filters_sem, energy_sem = ham_first + 2 * PLANE, ham_first + 2 * PLANE + 1

    def row_chunks(buf, send, group, sizes):
        return [
            Row(cp, me, buf, send, group * row_sems + c * ROW, sum(sizes[:c]), size) for c, size in enumerate(sizes)
        ]

    def drain_rows(buf, send):
        cp.sent(buf.at[:, : 7 * WIDE], send)

    hams = []
    for i in range(2):
        piece = tall_piece(hcol, i * (TALL // 2), TALL // 4)
        hams.append(Plane(cp, me, hcol, piece, TALL // 4, SLIM, 4 + i, ham_sems[i]))
    ham_tasks = {**hams[0].tasks("H"), **hams[1].tasks("I")}

    cp.send(filters, others, 6, filters_sem, me.partner())
    panel = colp.at[0]
    plane = Plane(cp, me, panel, tall_piece(panel, 0, TALL // 2, 1), TALL // 2, SLIM, 2, even_sems[0])
    whole = Row(cp, me, rowp, 0, 0, 0, ROWS)
    first = Product(rowp, panel)

    def whole_start():
        rowp[:, own_rows] = colp[0, mine]
        whole.start()

    tasks = {**plane.tasks("A"), **ham_tasks}
    tasks.update(R=whole_start, Ra=whole.arrive, Rs=whole.shared, E=lambda: first.blocks(me, EARLY))
    run(tasks, ORDER_A)
    plane.drain()
    cp.arrive(others, filters_sem)

    for step in range(2):
        drain_rows(rowp, 0)
        panel, after = colp.at[step], colp.at[1 - step]
        sizes = SIZES[step]
        count = len(sizes)
        chunk = [slice(sum(sizes[:c]), sum(sizes[: c + 1])) for c in range(count)]
        sems = odd_sems if step == 0 else even_sems
        pairs = []
        for i in range(0, count, 2):
            piece = chunk_piece(after, chunk[i].start, sizes[i])
            pairs.append(Plane(cp, me, after, piece, sizes[i], WIDE, 3 - step, sems[i // 2]))
        inner, rows = row_chunks(srow, 1, 1, sizes), row_chunks(rowp, 0, 0, sizes)
        last = row_chunks(grow, 7, 2, sizes)
        thirds = [Product(srow, panel, chunk[c].start, sizes[c]) for c in range(count)]
        own_piece, own_block = after.at[mine], rowp.at[:, own_rows]
        blocks = [filters[step].astype(F32), others[step].astype(F32)]
        keep = [jnp.where(me.zl == 0, m[:, :4], m[:, 4:]) for m in blocks]
        left = jnp.where(me.zl == 0, keep[0], keep[1])
        right = jnp.where(me.zl == 0, keep[1], keep[0])
        early = first.total
        cut = chunk[-1].start
        upper, lower = Product(grow, after, 0, cut), Product(grow, after, cut, sizes[-1])

        def square_chunk(c):
            tail = Product(rowp, panel, chunk[c].start, sizes[c])
            tail.total = early[chunk[c]]
            tail.blocks(me, LATE)
            srow[chunk[c], own_rows] = tail.total.astype(BF)
            inner[c].start()
            square[chunk[c]] = tail.total

        def third_chunk(c):
            inner[c].arrive()
            thirds[c].tiles(me, 0, 0, 1, 3, 2)

        def dens_chunk(c):
            inner[c].shared()
            thirds[c].tiles(me, 1, 0, 1, 3, 2)
            lo = chunk[c].start
            while lo < chunk[c].stop:
                hi = min(lo // BS * BS + BS, chunk[c].stop)
                mask = jnp.concatenate([mask_row(left, lo // BS), mask_row(right, lo // BS)], axis=1)
                third = thirds[c].total[lo - chunk[c].start : hi - chunk[c].start]
                dens = (mask * (3.0 * square[lo:hi] - 2.0 * third)).astype(BF)
                own_piece[lo:hi] = dens
                own_block[lo:hi] = dens
                lo = hi

        def rows_start(c):
            if c == count - 1:
                drain_rows(srow, 1)
            rows[c].start()

        def inward(c):
            part = Product(rowp, hcol, chunk[c].start, sizes[c])
            part.tiles(me, 0, 0, 1, 3, 2)
            part.tiles(me, 1, 0, 1, 3, 2)
            grow[chunk[c], own_rows] = part.total.astype(BF)
            last[c].start()

        def give(lo, hi):
            for owner in range(lo // OWN, hi // OWN):
                src = etile.at[owner * OWN : (owner + 1) * OWN]
                target = me.at(owner // 2, me.y, me.z, owner % 2)

                @pl.when(me.own != owner)
                def _():
                    cp.send(src, eall.at[:, own_rows], 8, energy_sem, target)

        def energy_upper():
            for dk in range(2):
                upper.tiles(me, dk, 0, 1, 3, 2)
            etile[:cut] = upper.total.astype(BF)
            give(0, cut)

        def energy_lower():
            for dk in range(2):
                lower.tiles(me, dk, 0, 1, 3, 2)
            etile[cut:] = lower.total.astype(BF)
            give(cut, ROWS)

        tasks = dict(ham_tasks)
        for name, pair in zip("PQW", pairs):
            tasks.update(pair.tasks(name))
        steps = dict(S=square_chunk, T=third_chunk, D=dens_chunk, R=rows_start, G=inward)
        for c in range(count):
            tasks.update({name + str(c): functools.partial(f, c) for name, f in steps.items()})
            tasks.update({"Ra" + str(c): rows[c].arrive, "Rs" + str(c): rows[c].shared})
            tasks.update({"La" + str(c): last[c].arrive, "Ls" + str(c): last[c].shared})
        if step == 0:
            first = Product(rowp, after)
            tasks.update(E=functools.partial(first.blocks, me, EARLY))
        tasks.update(U=energy_upper, V=energy_lower)
        run(tasks, ORDER_B if step == 0 else ORDER_C)
        cp.sent(after.at[: 15 * ROWS], 3 - step)

    for ham in hams:
        ham.drain()
    drain_rows(rowp, 0)
    drain_rows(grow, 7)
    eall[:, own_rows] = etile[pl.ds(pl.multiple_of(me.own * OWN, OWN), OWN)]
    same = lax.broadcasted_iota(jnp.int32, (OWN, OWN), 0) == lax.broadcasted_iota(jnp.int32, (OWN, OWN), 1)
    loads[4].wait()
    loads[5].wait()
    atom_of = jnp.sum(jnp.where(same, atoms[...].astype(F32), 0.0), axis=1, keepdims=True)
    cp.sent(filters, 6)
    cp.arrive(eall.at[:, : 7 * WIDE], energy_sem)
    for b in range(8):
        for zl in range(2):
            energy_out[:, (zl * 8 + b) * SLIM : (zl * 8 + b + 1) * SLIM] = eall[
                :, b * WIDE + zl * SLIM : b * WIDE + (zl + 1) * SLIM
            ]
    wide = energy_out[...].astype(F32)
    line = lax.broadcasted_iota(jnp.int32, (3, ATOM_DEV), 0)
    lane = lax.broadcasted_iota(jnp.int32, (3, ATOM_DEV), 1)
    forces = jnp.zeros((3, ATOM_DEV), F32)
    for axis in range(3):
        per_row = jnp.sum(deriv[axis].astype(F32) * wide, axis=1, keepdims=True)
        for atom in range(ATOM_DEV):
            force = jnp.sum(jnp.where(atom_of == atom, per_row, 0.0))
            forces = jnp.where((line == axis) & (lane == atom), force, forces)
    forces_out[...] = forces
    cp.sent(eall.at[:, : 7 * WIDE], 8)


def body(hamil, guess, pattern, filters, deriv, atom_of_row):
    args = (hamil, guess, pattern.T, filters.transpose(0, 2, 1), deriv, atom_of_row.reshape(1, OWN))
    vmem = pl.BlockSpec(memory_space=pltpu.VMEM)
    sems = 3 * max(map(len, SIZES)) * ROW + (sum(map(len, SIZES)) // 2 + 2) * PLANE + 2
    return pl.pallas_call(
        kernel,
        out_shape=(
            jax.ShapeDtypeStruct((OWN, N), BF),
            jax.ShapeDtypeStruct((3, ATOM_DEV), F32),
        ),
        in_specs=[pl.BlockSpec(memory_space=pl.ANY)] * 6,
        out_specs=(vmem, vmem),
        scratch_shapes=[pltpu.VMEM(arg.shape, arg.dtype) for arg in args]
        + [
            pltpu.VMEM((ROWS, N), BF),
            pltpu.VMEM((2, N, WIDE), BF),
            pltpu.VMEM((ROWS, N), BF),
            pltpu.VMEM((ROWS, N), BF),
            pltpu.VMEM((N, WIDE), BF),
            pltpu.VMEM((ROWS, WIDE), F32),
            pltpu.VMEM((ROWS, WIDE), BF),
            pltpu.VMEM((OWN, N), BF),
            pltpu.VMEM(args[3].shape, args[3].dtype),
            pltpu.SemaphoreType.DMA((6,)),
            pltpu.SemaphoreType.DMA((9,)),
            pltpu.SemaphoreType.DMA((sems,)),
        ],
        compiler_params=pltpu.CompilerParams(
            collective_id=0, has_side_effects=True, vmem_limit_bytes=60 * 1024 * 1024
        ),
    )(*args)


def solution(mesh):
    return jax.shard_map(
        body,
        mesh=mesh,
        in_specs=(
            P("row", "col"),
            P("row", "col"),
            P("row", "col"),
            P(None, "row", "col"),
            P(None, ("row", "col"), None),
            P(("row", "col")),
        ),
        out_specs=(P(("row", "col"), None), P(None, ("row", "col"))),
        check_vma=False,
    )
```

```python
import functools

import jax
import jax.numpy as jnp
from jax import lax
from jax.experimental import pallas as pl
from jax.experimental.pallas import tpu as pltpu
from jax.sharding import PartitionSpec as P

MESH = pl.DeviceIdType.MESH
BF, F32 = jnp.bfloat16, jnp.float32
BS = 64
ATOM_DEV = 4
N, OWN = 4096, 32
TALL, SLIM = 512, 256
ROWS, WIDE = 256, 512
SIZES = [[64, 64, 64, 64], [64, 64, 64, 64]]
PLANE, ROW = 16, 3


class Place:
    def __init__(self):
        row, col = lax.axis_index("row"), lax.axis_index("col")
        self.row, self.col = row, col
        self.zl = col // 8
        self.x, self.y, self.z, self.k = (col // 2) % 4, row // 2, (row % 2) * 2 + col // 8, col % 2
        self.own = self.x * 2 + self.k

    def at(self, x, y, z, k):
        return (y * 2 + z // 2, (z % 2) * 8 + x * 2 + k)

    def by(self, dx=0, dy=0, dz=0, dk=0):
        return self.at((self.x + dx) % 4, (self.y + dy) % 4, (self.z + dz) % 4, (self.k + dk) % 2)

    def partner(self):
        return (self.row, (self.col + 8) % 16)

    def line(self, dx, dk=0):
        return (self.x + dx) % 4 * 2 + (self.k + dk) % 2


class Copies:
    def __init__(self, me, send_sems, recv_sems):
        self.send_sems, self.recv_sems, self.any = send_sems, recv_sems, me.by(dx=1)

    def make(self, src, dst, send, recv, device):
        return pltpu.make_async_remote_copy(
            src_ref=src,
            dst_ref=dst,
            send_sem=self.send_sems.at[send],
            recv_sem=self.recv_sems.at[recv],
            device_id=device,
            device_id_type=MESH,
        )

    def send(self, src, dst, send, recv, device):
        self.make(src, dst, send, recv, device).start()

    def arrive(self, ref, recv):
        self.make(ref, ref, 0, recv, self.any).wait_recv()

    def sent(self, ref, send):
        self.make(ref, ref, send, 0, self.any).wait_send()


def chunk_piece(buf, first, rows):
    def piece(y, z, t, lo, size):
        start = (y * 4 + z) * ROWS + first + t * rows + lo
        return buf.at[pl.ds(pl.multiple_of(start, 16), size)]

    return piece


def tall_piece(buf, first, rows, swap=0):
    def piece(y, z, t, lo, size):
        start = (y * 2 + z // 2) * TALL + first + (t + swap * z) % 2 * rows + lo
        return buf.at[
            pl.ds(pl.multiple_of(start, 64), size), pl.ds(pl.multiple_of(z % 2 * SLIM, SLIM), SLIM)
        ]

    return piece


class Plane:
    def __init__(self, cp, me, buf, piece, rows, width, send, recv):
        self.cp, self.me, self.buf, self.piece = cp, me, buf, piece
        self.rows, self.send, self.recv = rows, send, recv
        self.equal = rows * width // WIDE

    def ref(self, t, i, j, lo=0, size=None):
        back = (i, j) if t == 0 else (j, i)
        y, z = (self.me.y + 4 - back[0]) % 4, (self.me.z + 4 - back[1]) % 4
        return self.piece(y, z, t, lo, self.rows if size is None else size)

    def put(self, t, i, j, axis, d, sem, lo=0, size=None):
        ref = self.ref(t, i, j, lo, size)
        device = self.me.by(dy=d) if axis == t else self.me.by(dz=d)
        self.cp.send(ref, ref, self.send, self.recv + sem, device)

    def got(self, sem, pieces=1):
        self.cp.arrive(self.buf.at[: pieces * self.equal], self.recv + sem)

    def own_first(self, t):
        self.put(t, 0, 0, 0, 1, 7 * t)
        self.put(t, 0, 0, 0, 3, 7 * t + 1)

    def own_second(self, t):
        self.put(t, 0, 0, 1, 1, 7 * t + 3)
        self.put(t, 0, 0, 1, 3, 7 * t + 3)

    def ring(self, t):
        half = self.rows // 2
        self.got(7 * t)
        self.put(t, 1, 0, 0, 1, 7 * t + 2, 0, half)
        self.got(7 * t + 1)
        self.put(t, 3, 0, 0, 3, 7 * t + 2, half, half)

    def spread(self, t):
        self.put(t, 1, 0, 1, 3, 7 * t + 4)
        self.put(t, 3, 0, 1, 1, 7 * t + 5)
        self.put(t, 1, 0, 1, 1, 14)
        self.put(t, 3, 0, 1, 3, 14)

    def own_far(self, t):
        self.got(7 * t + 3, 2)
        self.put(t, 0, 1, 1, 1, 15)

    def spread_far(self, t):
        self.got(7 * t + 2)
        self.put(t, 2, 0, 1, 3, 7 * t + 6)
        self.put(t, 2, 0, 1, 1, 14)

    def left_far(self, t):
        self.got(7 * t + 4)
        self.put(t, 1, 3, 1, 3, 15)

    def right_far(self, t):
        self.got(7 * t + 5)
        self.put(t, 3, 1, 1, 1, 15)

    def far_far(self, t):
        self.got(7 * t + 6)
        self.put(t, 2, 3, 1, 3, 15)

    def tasks(self, name):
        steps = [self.own_first, self.own_second, self.ring, self.spread, self.own_far]
        steps += [self.spread_far, self.left_far, self.right_far, self.far_far]
        out = {name + str(t) + l: functools.partial(f, t) for l, f in zip("abcdefghi", steps) for t in range(2)}
        return {**out, name + "n": self.near, name + "z": self.far}

    def near(self):
        self.got(14, 6)

    def far(self):
        self.got(15, 8)

    def drain(self):
        self.cp.sent(self.buf.at[: 30 * self.equal], self.send)


class Row:
    def __init__(self, cp, me, buf, send, recv, lo, size):
        self.cp, self.me, self.buf, self.send, self.recv = cp, me, buf, send, recv
        self.lo, self.size = lo, size

    def put(self, d, to, sem, dk=0):
        at = pl.multiple_of(self.me.line(4 - d) * WIDE, WIDE)
        ref = self.buf.at[self.lo : self.lo + self.size, pl.ds(at, WIDE)]
        self.cp.send(ref, ref, self.send, self.recv + sem, self.me.by(dx=to, dk=dk))

    def got(self, sem, tiles=1):
        self.cp.arrive(self.buf.at[: self.size, : tiles * WIDE], self.recv + sem)

    def start(self):
        self.put(0, 1, 0)
        self.put(0, 3, 0)
        self.put(0, 2, 1)
        self.put(0, 0, 2, dk=1)

    def arrive(self):
        self.got(0, 2)
        self.put(1, 0, 2, dk=1)
        self.put(3, 0, 2, dk=1)
        self.got(1)
        self.put(2, 0, 2, dk=1)

    def shared(self):
        self.got(2, 4)


def dot(a, b):
    return jnp.dot(a, b, preferred_element_type=F32)


def block_k(b, zl):
    return pl.ds(pl.multiple_of((zl * 8 + b) * ROWS, ROWS), ROWS)


class Product:
    def __init__(self, left, right, lo=0, size=ROWS):
        self.left, self.right, self.rows, self.total = left, right, slice(lo, lo + size), None

    def add(self, b, zl):
        at = pl.ds(pl.multiple_of(b * WIDE + zl * SLIM, SLIM), SLIM)
        term = dot(self.left[self.rows, at], self.right[block_k(b, zl)])
        self.total = term if self.total is None else self.total + term

    def tiles(self, me, dk, *ds):
        for d in ds:
            for zl in range(2):
                self.add(me.line(4 - d, dk), zl)

    def blocks(self, me, pairs):
        for dy, dz in pairs:
            r = (me.y + 4 - dy) % 4 * 4 + (me.z + 4 - dz) % 4
            self.add(r % 8, r // 8)


EARLY = [(dy, dz) for dy in (0, 1, 3) for dz in (0, 1, 3)]
LATE = [(d, 2) for d in range(4)] + [(2, d) for d in (0, 1, 3)]


def mask_row(blocks, i):
    count = blocks.shape[0]
    lane = lax.broadcasted_iota(jnp.int32, (1, count * BS), 1) // BS
    row = jnp.zeros((1, count * BS), F32)
    for j in range(count):
        row = jnp.where(lane == j, blocks[j : j + 1, i : i + 1], row)
    return row


def run(tasks, order):
    for name in order:
        tasks[name]()


ORDER_A = [
    "A1a", "A0a", "A1b", "A0b", "A1c", "A0c", "A1d", "A0d", "R", "A0f", "A1f", "A0e", "A0h", "A1e", "A1h", "A0g",
    "A1g", "A0i", "A1i", "An", "H1a", "Ra", "H0a", "H0b", "Rs", "H1b", "E", "Az",
]
ORDER_B = [
    "S0", "H1c", "H0c", "H0d", "S1", "H1d", "S2", "S3", "H1f", "H1g", "T0", "H1h", "H0e", "H0g", "H0f", "D0", "P0a",
    "T1", "H1i", "H1e", "P0b", "D1", "P1a", "T2", "P1b", "P0c", "P0d", "D2", "Q0a", "Hn", "T3", "P1c", "P1d", "Q0b",
    "R0", "D3", "R3", "Q1a", "Q0c", "P0f", "Q1b", "H0h", "H0i", "P1f", "R1", "R2", "Q1c", "Q1d", "Q0f", "Q0d",
    "P0g", "Q0e", "P0h", "P1i", "P1e", "P0i", "Q1f", "P0e", "Ra0", "Ra1", "Q1h", "P1g", "Hz", "Q0h", "P1h", "Ra3",
    "Q0g", "Rs0", "Q1g", "Q0i", "I1a", "Q1e", "Pn", "Q1i", "Ra2", "Qn", "I0a", "Pz", "Rs3", "Rs1", "Rs2", "I0b",
    "I1b", "E", "Qz",
]
ORDER_C = [
    "S0", "I1c", "I0c", "I1d", "I0d", "S1", "I1f", "S2", "I0f", "T0", "I0e", "I1e", "I1g", "I0g", "S3", "I0h", "D0",
    "I1h", "P0a", "P0b", "T1", "I0i", "D1", "R1", "P1a", "I1i", "T2", "P1b", "R0", "D2", "Q0b", "Q0a", "R2", "T3",
    "P1c", "P1d", "P0c", "In", "D3", "Q1a", "P0d", "Q1b", "R3", "Ra1", "Q0c", "Rs1", "Iz", "Go1", "G1", "Q1c",
    "P1h", "Ra0", "Q0d", "P1f", "Go0", "Rs0", "Q1d", "G0", "Ra2", "P0f", "Q1f", "Q0f", "P0e", "Q0h", "Go2", "Rs2",
    "Q0g", "Q1e", "P1g", "Ra3", "Q0e", "P0g", "P1e", "G2", "Q1g", "Q1h", "P0i", "P1i", "Go3", "Rs3", "G3", "La1",
    "Q1i", "Q0i", "P0h", "La0", "Qn", "La2", "Ls1", "Ls0", "Pn", "Qz", "Pz", "Ls2", "U", "La3", "Vo", "Ls3", "V",
]


def kernel(
    hamil_hbm, guess_hbm, pattern_hbm, filters_hbm, deriv_hbm, atoms_hbm,
    energy_out, forces_out,
    hamil, guess, pattern, filters, deriv, atoms,
    rowp, colp, srow, grow, hcol, square, etile, eall, others, load_sems, send_sems, recv_sems,
):
    me = Place()
    cp = Copies(me, send_sems, recv_sems)
    peers = [me.by(dx=dx, dk=dk) for dx in range(4) for dk in range(2)][1:]
    peers += [me.by(dy=1), me.by(dy=3), me.by(dz=1), me.by(dz=3)]
    barrier = pltpu.get_barrier_semaphore()
    for peer in peers:
        pl.semaphore_signal(barrier, inc=1, device_id=peer, device_id_type=MESH)

    pairs = [(pattern_hbm, pattern), (guess_hbm, guess), (hamil_hbm, hamil)]
    pairs += [(filters_hbm, filters), (deriv_hbm, deriv), (atoms_hbm, atoms)]
    loads = [pltpu.make_async_copy(a, b, load_sems.at[i]) for i, (a, b) in enumerate(pairs)]
    for load in loads:
        load.start()
    for load in loads[:4]:
        load.wait()

    tall = pl.ds(pl.multiple_of(me.row * TALL, TALL), TALL)
    slim = pl.ds(pl.multiple_of(me.zl * SLIM, SLIM), SLIM)
    own_guess, own_ham = colp.at[0].at[tall, slim], hcol.at[tall, slim]
    kept = pattern[...].astype(F32)
    for i in range(TALL // BS):
        part = slice(i * BS, (i + 1) * BS)
        keep = mask_row(kept, i)
        here = me.row * TALL + i * BS + lax.broadcasted_iota(jnp.int32, (BS, SLIM), 0)
        there = me.col * SLIM + lax.broadcasted_iota(jnp.int32, (BS, SLIM), 1)
        half = jnp.where(here == there, 0.5, 0.0).astype(F32)
        own_guess[part] = ((half + guess[part].astype(F32)) * keep).astype(BF)
        own_ham[part] = jnp.where(keep > 0, hamil[part].astype(F32), 0.0).astype(BF)
    pl.semaphore_wait(barrier, len(peers))

    mine = pl.ds(pl.multiple_of((me.y * 4 + me.z) * ROWS, ROWS), ROWS)
    own_rows = pl.ds(pl.multiple_of(me.own * WIDE, WIDE), WIDE)
    row_sems = max(map(len, SIZES)) * ROW
    planes = 3 * row_sems
    odd_sems = [planes + i * PLANE for i in range(len(SIZES[0]) // 2)]
    even_sems = [planes + (len(odd_sems) + i) * PLANE for i in range(len(SIZES[1]) // 2)]
    ham_first = planes + (len(odd_sems) + len(even_sems)) * PLANE
    ham_sems = [ham_first, ham_first + PLANE]
    filters_sem, energy_sem = ham_first + 2 * PLANE, ham_first + 2 * PLANE + 1

    def row_chunks(buf, send, group, sizes):
        return [
            Row(cp, me, buf, send, group * row_sems + c * ROW, sum(sizes[:c]), size) for c, size in enumerate(sizes)
        ]

    def drain_rows(buf, send):
        cp.sent(buf.at[:, : 7 * WIDE], send)

    hams = []
    for i in range(2):
        piece = tall_piece(hcol, i * (TALL // 2), TALL // 4)
        hams.append(Plane(cp, me, hcol, piece, TALL // 4, SLIM, 4 + i, ham_sems[i]))
    ham_tasks = {**hams[0].tasks("H"), **hams[1].tasks("I")}

    cp.send(filters, others, 6, filters_sem, me.partner())
    panel = colp.at[0]
    plane = Plane(cp, me, panel, tall_piece(panel, 0, TALL // 2, 1), TALL // 2, SLIM, 2, even_sems[0])
    whole = Row(cp, me, rowp, 0, 0, 0, ROWS)
    first = Product(rowp, panel)

    def whole_start():
        rowp[:, own_rows] = colp[0, mine]
        whole.start()

    tasks = {**plane.tasks("A"), **ham_tasks}
    tasks.update(R=whole_start, Ra=whole.arrive, Rs=whole.shared, E=lambda: first.blocks(me, EARLY))
    run(tasks, ORDER_A)
    plane.drain()
    cp.arrive(others, filters_sem)

    for step in range(2):
        drain_rows(rowp, 0)
        panel, after = colp.at[step], colp.at[1 - step]
        sizes = SIZES[step]
        count = len(sizes)
        chunk = [slice(sum(sizes[:c]), sum(sizes[: c + 1])) for c in range(count)]
        sems = odd_sems if step == 0 else even_sems
        pairs = []
        for i in range(0, count, 2):
            piece = chunk_piece(after, chunk[i].start, sizes[i])
            pairs.append(Plane(cp, me, after, piece, sizes[i], WIDE, 3 - step, sems[i // 2]))
        inner, rows = row_chunks(srow, 1, 1, sizes), row_chunks(rowp, 0, 0, sizes)
        last = row_chunks(grow, 7, 2, sizes)
        thirds = [Product(srow, panel, chunk[c].start, sizes[c]) for c in range(count)]
        inwards = [Product(rowp, hcol, chunk[c].start, sizes[c]) for c in range(count)]
        own_piece, own_block = after.at[mine], rowp.at[:, own_rows]
        blocks = [filters[step].astype(F32), others[step].astype(F32)]
        keep = [jnp.where(me.zl == 0, m[:, :4], m[:, 4:]) for m in blocks]
        left = jnp.where(me.zl == 0, keep[0], keep[1])
        right = jnp.where(me.zl == 0, keep[1], keep[0])
        early = first.total
        cut = chunk[-1].start
        upper, lower = Product(grow, after, 0, cut), Product(grow, after, cut, sizes[-1])

        def square_chunk(c):
            tail = Product(rowp, panel, chunk[c].start, sizes[c])
            tail.total = early[chunk[c]]
            tail.blocks(me, LATE)
            srow[chunk[c], own_rows] = tail.total.astype(BF)
            inner[c].start()
            square[chunk[c]] = tail.total

        def third_chunk(c):
            inner[c].arrive()
            thirds[c].tiles(me, 0, 0, 1, 3, 2)

        def dens_chunk(c):
            inner[c].shared()
            thirds[c].tiles(me, 1, 0, 1, 3, 2)
            lo = chunk[c].start
            while lo < chunk[c].stop:
                hi = min(lo // BS * BS + BS, chunk[c].stop)
                mask = jnp.concatenate([mask_row(left, lo // BS), mask_row(right, lo // BS)], axis=1)
                third = thirds[c].total[lo - chunk[c].start : hi - chunk[c].start]
                dens = (mask * (3.0 * square[lo:hi] - 2.0 * third)).astype(BF)
                own_piece[lo:hi] = dens
                own_block[lo:hi] = dens
                lo = hi

        def rows_start(c):
            if c == count - 1:
                drain_rows(srow, 1)
            rows[c].start()

        def inward_own(c):
            inwards[c].tiles(me, 0, 0, 1, 3, 2)

        def inward(c):
            inwards[c].tiles(me, 1, 0, 1, 3, 2)
            grow[chunk[c], own_rows] = inwards[c].total.astype(BF)
            last[c].start()

        def give(lo, hi):
            for owner in range(lo // OWN, hi // OWN):
                src = etile.at[owner * OWN : (owner + 1) * OWN]
                target = me.at(owner // 2, me.y, me.z, owner % 2)

                @pl.when(me.own != owner)
                def _():
                    cp.send(src, eall.at[:, own_rows], 8, energy_sem, target)

        def energy_upper():
            for dk in range(2):
                upper.tiles(me, dk, 0, 1, 3, 2)
            etile[:cut] = upper.total.astype(BF)
            give(0, cut)

        def energy_lower_own():
            lower.tiles(me, 0, 0, 1, 3, 2)

        def energy_lower():
            lower.tiles(me, 1, 0, 1, 3, 2)
            etile[cut:] = lower.total.astype(BF)
            give(cut, ROWS)

        tasks = dict(ham_tasks)
        for name, pair in zip("PQW", pairs):
            tasks.update(pair.tasks(name))
        steps = dict(S=square_chunk, T=third_chunk, D=dens_chunk, R=rows_start, Go=inward_own, G=inward)
        for c in range(count):
            tasks.update({name + str(c): functools.partial(f, c) for name, f in steps.items()})
            tasks.update({"Ra" + str(c): rows[c].arrive, "Rs" + str(c): rows[c].shared})
            tasks.update({"La" + str(c): last[c].arrive, "Ls" + str(c): last[c].shared})
        if step == 0:
            first = Product(rowp, after)
            tasks.update(E=functools.partial(first.blocks, me, EARLY))
        tasks.update(U=energy_upper, Vo=energy_lower_own, V=energy_lower)
        run(tasks, ORDER_B if step == 0 else ORDER_C)
        cp.sent(after.at[: 15 * ROWS], 3 - step)

    for ham in hams:
        ham.drain()
    drain_rows(rowp, 0)
    drain_rows(grow, 7)
    eall[:, own_rows] = etile[pl.ds(pl.multiple_of(me.own * OWN, OWN), OWN)]
    same = lax.broadcasted_iota(jnp.int32, (OWN, OWN), 0) == lax.broadcasted_iota(jnp.int32, (OWN, OWN), 1)
    loads[4].wait()
    loads[5].wait()
    atom_of = jnp.sum(jnp.where(same, atoms[...].astype(F32), 0.0), axis=1, keepdims=True)
    cp.sent(filters, 6)
    cp.arrive(eall.at[:, : 7 * WIDE], energy_sem)
    for b in range(8):
        for zl in range(2):
            energy_out[:, (zl * 8 + b) * SLIM : (zl * 8 + b + 1) * SLIM] = eall[
                :, b * WIDE + zl * SLIM : b * WIDE + (zl + 1) * SLIM
            ]
    wide = energy_out[...].astype(F32)
    line = lax.broadcasted_iota(jnp.int32, (3, ATOM_DEV), 0)
    lane = lax.broadcasted_iota(jnp.int32, (3, ATOM_DEV), 1)
    forces = jnp.zeros((3, ATOM_DEV), F32)
    for axis in range(3):
        per_row = jnp.sum(deriv[axis].astype(F32) * wide, axis=1, keepdims=True)
        for atom in range(ATOM_DEV):
            force = jnp.sum(jnp.where(atom_of == atom, per_row, 0.0))
            forces = jnp.where((line == axis) & (lane == atom), force, forces)
    forces_out[...] = forces
    cp.sent(eall.at[:, : 7 * WIDE], 8)


def body(hamil, guess, pattern, filters, deriv, atom_of_row):
    args = (hamil, guess, pattern.T, filters.transpose(0, 2, 1), deriv, atom_of_row.reshape(1, OWN))
    vmem = pl.BlockSpec(memory_space=pltpu.VMEM)
    sems = 3 * max(map(len, SIZES)) * ROW + (sum(map(len, SIZES)) // 2 + 2) * PLANE + 2
    return pl.pallas_call(
        kernel,
        out_shape=(
            jax.ShapeDtypeStruct((OWN, N), BF),
            jax.ShapeDtypeStruct((3, ATOM_DEV), F32),
        ),
        in_specs=[pl.BlockSpec(memory_space=pl.ANY)] * 6,
        out_specs=(vmem, vmem),
        scratch_shapes=[pltpu.VMEM(arg.shape, arg.dtype) for arg in args]
        + [
            pltpu.VMEM((ROWS, N), BF),
            pltpu.VMEM((2, N, WIDE), BF),
            pltpu.VMEM((ROWS, N), BF),
            pltpu.VMEM((ROWS, N), BF),
            pltpu.VMEM((N, WIDE), BF),
            pltpu.VMEM((ROWS, WIDE), F32),
            pltpu.VMEM((ROWS, WIDE), BF),
            pltpu.VMEM((OWN, N), BF),
            pltpu.VMEM(args[3].shape, args[3].dtype),
            pltpu.SemaphoreType.DMA((6,)),
            pltpu.SemaphoreType.DMA((9,)),
            pltpu.SemaphoreType.DMA((sems,)),
        ],
        compiler_params=pltpu.CompilerParams(
            collective_id=0, has_side_effects=True, vmem_limit_bytes=60 * 1024 * 1024
        ),
    )(*args)


def solution(mesh):
    return jax.shard_map(
        body,
        mesh=mesh,
        in_specs=(
            P("row", "col"),
            P("row", "col"),
            P("row", "col"),
            P(None, "row", "col"),
            P(None, ("row", "col"), None),
            P(("row", "col")),
        ),
        out_specs=(P(("row", "col"), None), P(None, ("row", "col"))),
        check_vma=False,
    )
```

```python
import functools

import jax
import jax.numpy as jnp
from jax import lax
from jax.experimental import pallas as pl
from jax.experimental.pallas import tpu as pltpu
from jax.sharding import PartitionSpec as P

MESH = pl.DeviceIdType.MESH
BF, F32 = jnp.bfloat16, jnp.float32
BS = 64
ATOM_DEV = 4
N, OWN = 4096, 32
TALL, SLIM = 512, 256
ROWS, WIDE = 256, 512
SIZES = [[64, 64, 64, 64], [64, 64, 64, 64]]
PLANE, ROW = 16, 3


class Place:
    def __init__(self):
        row, col = lax.axis_index("row"), lax.axis_index("col")
        self.row, self.col = row, col
        self.zl = col // 8
        self.x, self.y, self.z, self.k = (col // 2) % 4, row // 2, (row % 2) * 2 + col // 8, col % 2
        self.own = self.x * 2 + self.k

    def at(self, x, y, z, k):
        return (y * 2 + z // 2, (z % 2) * 8 + x * 2 + k)

    def by(self, dx=0, dy=0, dz=0, dk=0):
        return self.at((self.x + dx) % 4, (self.y + dy) % 4, (self.z + dz) % 4, (self.k + dk) % 2)

    def partner(self):
        return (self.row, (self.col + 8) % 16)

    def line(self, dx, dk=0):
        return (self.x + dx) % 4 * 2 + (self.k + dk) % 2


class Copies:
    def __init__(self, me, send_sems, recv_sems):
        self.send_sems, self.recv_sems, self.any = send_sems, recv_sems, me.by(dx=1)

    def make(self, src, dst, send, recv, device):
        return pltpu.make_async_remote_copy(
            src_ref=src,
            dst_ref=dst,
            send_sem=self.send_sems.at[send],
            recv_sem=self.recv_sems.at[recv],
            device_id=device,
            device_id_type=MESH,
        )

    def send(self, src, dst, send, recv, device):
        self.make(src, dst, send, recv, device).start()

    def arrive(self, ref, recv):
        self.make(ref, ref, 0, recv, self.any).wait_recv()

    def sent(self, ref, send):
        self.make(ref, ref, send, 0, self.any).wait_send()


def chunk_piece(buf, first, rows):
    def piece(y, z, t, lo, size):
        start = (y * 4 + z) * ROWS + first + t * rows + lo
        return buf.at[pl.ds(pl.multiple_of(start, 16), size)]

    return piece


def tall_piece(buf, first, rows, swap=0):
    def piece(y, z, t, lo, size):
        start = (y * 2 + z // 2) * TALL + first + (t + swap * z) % 2 * rows + lo
        return buf.at[
            pl.ds(pl.multiple_of(start, 64), size), pl.ds(pl.multiple_of(z % 2 * SLIM, SLIM), SLIM)
        ]

    return piece


class Plane:
    def __init__(self, cp, me, buf, piece, rows, width, send, recv):
        self.cp, self.me, self.buf, self.piece = cp, me, buf, piece
        self.rows, self.send, self.recv = rows, send, recv
        self.equal = rows * width // WIDE

    def ref(self, t, i, j, lo=0, size=None):
        back = (i, j) if t == 0 else (j, i)
        y, z = (self.me.y + 4 - back[0]) % 4, (self.me.z + 4 - back[1]) % 4
        return self.piece(y, z, t, lo, self.rows if size is None else size)

    def put(self, t, i, j, axis, d, sem, lo=0, size=None):
        ref = self.ref(t, i, j, lo, size)
        device = self.me.by(dy=d) if axis == t else self.me.by(dz=d)
        self.cp.send(ref, ref, self.send, self.recv + sem, device)

    def got(self, sem, pieces=1):
        self.cp.arrive(self.buf.at[: pieces * self.equal], self.recv + sem)

    def own_first(self, t):
        self.put(t, 0, 0, 0, 1, 7 * t)
        self.put(t, 0, 0, 0, 3, 7 * t + 1)

    def own_second(self, t):
        self.put(t, 0, 0, 1, 1, 7 * t + 3)
        self.put(t, 0, 0, 1, 3, 7 * t + 3)

    def ring(self, t):
        half = self.rows // 2
        self.got(7 * t)
        self.put(t, 1, 0, 0, 1, 7 * t + 2, 0, half)
        self.got(7 * t + 1)
        self.put(t, 3, 0, 0, 3, 7 * t + 2, half, half)

    def spread(self, t):
        self.put(t, 1, 0, 1, 3, 7 * t + 4)
        self.put(t, 3, 0, 1, 1, 7 * t + 5)
        self.put(t, 1, 0, 1, 1, 14)
        self.put(t, 3, 0, 1, 3, 14)

    def own_far(self, t):
        self.got(7 * t + 3, 2)
        self.put(t, 0, 1, 1, 1, 15)

    def spread_far(self, t):
        self.got(7 * t + 2)
        self.put(t, 2, 0, 1, 3, 7 * t + 6)
        self.put(t, 2, 0, 1, 1, 14)

    def left_far(self, t):
        self.got(7 * t + 4)
        self.put(t, 1, 3, 1, 3, 15)

    def right_far(self, t):
        self.got(7 * t + 5)
        self.put(t, 3, 1, 1, 1, 15)

    def far_far(self, t):
        self.got(7 * t + 6)
        self.put(t, 2, 3, 1, 3, 15)

    def tasks(self, name):
        steps = [self.own_first, self.own_second, self.ring, self.spread, self.own_far]
        steps += [self.spread_far, self.left_far, self.right_far, self.far_far]
        out = {name + str(t) + l: functools.partial(f, t) for l, f in zip("abcdefghi", steps) for t in range(2)}
        return {**out, name + "n": self.near, name + "z": self.far}

    def near(self):
        self.got(14, 6)

    def far(self):
        self.got(15, 8)

    def drain(self):
        self.cp.sent(self.buf.at[: 30 * self.equal], self.send)


class Row:
    def __init__(self, cp, me, buf, send, recv, lo, size):
        self.cp, self.me, self.buf, self.send, self.recv = cp, me, buf, send, recv
        self.lo, self.size = lo, size

    def put(self, d, to, sem, dk=0):
        at = pl.multiple_of(self.me.line(4 - d) * WIDE, WIDE)
        ref = self.buf.at[self.lo : self.lo + self.size, pl.ds(at, WIDE)]
        self.cp.send(ref, ref, self.send, self.recv + sem, self.me.by(dx=to, dk=dk))

    def got(self, sem, tiles=1):
        self.cp.arrive(self.buf.at[: self.size, : tiles * WIDE], self.recv + sem)

    def start(self):
        self.put(0, 1, 0)
        self.put(0, 3, 0)
        self.put(0, 2, 1)
        self.put(0, 0, 2, dk=1)

    def arrive(self):
        self.got(0, 2)
        self.put(1, 0, 2, dk=1)
        self.put(3, 0, 2, dk=1)
        self.got(1)
        self.put(2, 0, 2, dk=1)

    def shared(self):
        self.got(2, 4)


def dot(a, b):
    return jnp.dot(a, b, preferred_element_type=F32)


def block_k(b, zl):
    return pl.ds(pl.multiple_of((zl * 8 + b) * ROWS, ROWS), ROWS)


class Product:
    def __init__(self, left, right, lo=0, size=ROWS):
        self.left, self.right, self.rows, self.total = left, right, slice(lo, lo + size), None

    def add(self, b, zl):
        at = pl.ds(pl.multiple_of(b * WIDE + zl * SLIM, SLIM), SLIM)
        term = dot(self.left[self.rows, at], self.right[block_k(b, zl)])
        self.total = term if self.total is None else self.total + term

    def tiles(self, me, dk, *ds):
        for d in ds:
            for zl in range(2):
                self.add(me.line(4 - d, dk), zl)

    def blocks(self, me, pairs):
        for dy, dz in pairs:
            r = (me.y + 4 - dy) % 4 * 4 + (me.z + 4 - dz) % 4
            self.add(r % 8, r // 8)


EARLY = [(dy, dz) for dy in (0, 1, 3) for dz in (0, 1, 3)]
LATE = [(d, 2) for d in range(4)] + [(2, d) for d in (0, 1, 3)]


def mask_row(blocks, i):
    count = blocks.shape[0]
    lane = lax.broadcasted_iota(jnp.int32, (1, count * BS), 1) // BS
    row = jnp.zeros((1, count * BS), F32)
    for j in range(count):
        row = jnp.where(lane == j, blocks[j : j + 1, i : i + 1], row)
    return row


def run(tasks, order):
    for name in order:
        tasks[name]()


ORDER_A = [
    "A1a", "A0a", "A1b", "A0b", "A1c", "A0c", "A1d", "A0d", "R", "A0f", "A1f", "A0e", "A0h", "A1e", "A1h", "A0g",
    "A1g", "A0i", "A1i", "An", "H1a", "Ra", "H0a", "H0b", "Rs", "H1b", "E", "Az",
]
ORDER_B = [
    "S0", "H1c", "H0c", "H0d", "S1", "H1d", "S2", "S3", "H1f", "H1g", "T0", "H1h", "H0e", "H0g", "H0f", "D0", "P0a",
    "T1", "H1i", "H1e", "P0b", "D1", "P1a", "T2", "P1b", "P0c", "P0d", "D2", "Q0a", "Hn", "T3", "P1c", "P1d", "Q0b",
    "R0", "D3", "R3", "Q1a", "Q0c", "P0f", "Q1b", "H0h", "H0i", "P1f", "R1", "R2", "Q1c", "Q1d", "Q0f", "Q0d",
    "P0g", "Q0e", "P0h", "P1i", "P1e", "P0i", "Q1f", "P0e", "Ra0", "Ra1", "Q1h", "P1g", "Hz", "Q0h", "P1h", "Ra3",
    "Q0g", "Rs0", "Q1g", "Q0i", "I1a", "Q1e", "Pn", "Q1i", "Ra2", "Qn", "I0a", "Pz", "Rs3", "Rs1", "Rs2", "I0b",
    "I1b", "E", "Qz",
]
ORDER_C = [
    "S0", "I1c", "I0c", "I1d", "I0d", "S1", "I1f", "S2", "I0f", "T0", "I0e", "I1e", "I1g", "I0g", "S3", "I0h", "D0",
    "I1h", "P0a", "P0b", "T1", "I0i", "D1", "R1", "P1a", "I1i", "T2", "P1b", "R0", "D2", "Q0b", "Q0a", "R2", "T3",
    "P1c", "P1d", "P0c", "In", "D3", "Q1a", "P0d", "Q1b", "R3", "Ra1", "Q0c", "Rs1", "Iz", "Go1", "G1", "Q1c",
    "P1h", "Ra0", "Q0d", "P1f", "Go0", "Rs0", "Q1d", "G0", "Ra2", "P0f", "Q1f", "Q0f", "P0e", "Q0h", "Go2", "Rs2",
    "Q0g", "Q1e", "P1g", "Ra3", "Q0e", "P0g", "P1e", "G2", "Q1g", "Q1h", "P0i", "P1i", "Go3", "Rs3", "G3", "La1",
    "Q1i", "Q0i", "P0h", "La0", "Qn", "La2", "Ls1", "Ls0", "Pn", "Qz", "Pz", "Ls2", "U", "La3", "Vo", "Ls3", "V",
]


def kernel(
    hamil_hbm, guess_hbm, pattern_hbm, filters_hbm, deriv_hbm, atoms_hbm,
    energy_out, forces_out,
    hamil, guess, pattern, filters, deriv, atoms,
    rowp, colp, srow, grow, hcol, square, etile, eall, others, load_sems, send_sems, recv_sems,
):
    me = Place()
    cp = Copies(me, send_sems, recv_sems)
    peers = [me.by(dx=dx, dk=dk) for dx in range(4) for dk in range(2)][1:]
    peers += [me.by(dy=1), me.by(dy=3), me.by(dz=1), me.by(dz=3)]
    barrier = pltpu.get_barrier_semaphore()
    for peer in peers:
        pl.semaphore_signal(barrier, inc=1, device_id=peer, device_id_type=MESH)

    pairs = [(pattern_hbm, pattern), (guess_hbm, guess), (hamil_hbm, hamil)]
    pairs += [(filters_hbm, filters), (deriv_hbm, deriv), (atoms_hbm, atoms)]
    loads = [pltpu.make_async_copy(a, b, load_sems.at[i]) for i, (a, b) in enumerate(pairs)]
    for load in loads:
        load.start()
    for load in loads[:4]:
        load.wait()

    tall = pl.ds(pl.multiple_of(me.row * TALL, TALL), TALL)
    slim = pl.ds(pl.multiple_of(me.zl * SLIM, SLIM), SLIM)
    own_guess, own_ham = colp.at[0].at[tall, slim], hcol.at[tall, slim]
    kept = pattern[...].astype(F32)
    for i in range(TALL // BS):
        part = slice(i * BS, (i + 1) * BS)
        keep = mask_row(kept, i)
        here = me.row * TALL + i * BS + lax.broadcasted_iota(jnp.int32, (BS, SLIM), 0)
        there = me.col * SLIM + lax.broadcasted_iota(jnp.int32, (BS, SLIM), 1)
        half = jnp.where(here == there, 0.5, 0.0).astype(F32)
        own_guess[part] = ((half + guess[part].astype(F32)) * keep).astype(BF)
        own_ham[part] = jnp.where(keep > 0, hamil[part].astype(F32), 0.0).astype(BF)
    pl.semaphore_wait(barrier, len(peers))

    mine = pl.ds(pl.multiple_of((me.y * 4 + me.z) * ROWS, ROWS), ROWS)
    own_rows = pl.ds(pl.multiple_of(me.own * WIDE, WIDE), WIDE)
    row_sems = max(map(len, SIZES)) * ROW
    planes = 3 * row_sems
    odd_sems = [planes + i * PLANE for i in range(len(SIZES[0]) // 2)]
    even_sems = [planes + (len(odd_sems) + i) * PLANE for i in range(len(SIZES[1]) // 2)]
    ham_first = planes + (len(odd_sems) + len(even_sems)) * PLANE
    ham_sems = [ham_first, ham_first + PLANE]
    filters_sem, energy_sem = ham_first + 2 * PLANE, ham_first + 2 * PLANE + 1

    def row_chunks(buf, send, group, sizes):
        return [
            Row(cp, me, buf, send, group * row_sems + c * ROW, sum(sizes[:c]), size) for c, size in enumerate(sizes)
        ]

    def drain_rows(buf, send):
        cp.sent(buf.at[:, : 7 * WIDE], send)

    hams = []
    for i in range(2):
        piece = tall_piece(hcol, i * (TALL // 2), TALL // 4)
        hams.append(Plane(cp, me, hcol, piece, TALL // 4, SLIM, 4 + i, ham_sems[i]))
    ham_tasks = {**hams[0].tasks("H"), **hams[1].tasks("I")}

    cp.send(filters, others, 6, filters_sem, me.partner())
    panel = colp.at[0]
    plane = Plane(cp, me, panel, tall_piece(panel, 0, TALL // 2, 1), TALL // 2, SLIM, 2, even_sems[0])
    whole = Row(cp, me, rowp, 0, 0, 0, ROWS)
    first = Product(rowp, panel)

    def whole_start():
        rowp[:, own_rows] = colp[0, mine]
        whole.start()

    tasks = {**plane.tasks("A"), **ham_tasks}
    tasks.update(R=whole_start, Ra=whole.arrive, Rs=whole.shared, E=lambda: first.blocks(me, EARLY))
    run(tasks, ORDER_A)
    plane.drain()
    cp.arrive(others, filters_sem)

    for step in range(2):
        drain_rows(rowp, 0)
        panel, after = colp.at[step], colp.at[1 - step]
        sizes = SIZES[step]
        count = len(sizes)
        chunk = [slice(sum(sizes[:c]), sum(sizes[: c + 1])) for c in range(count)]
        sems = odd_sems if step == 0 else even_sems
        pairs = []
        for i in range(0, count, 2):
            piece = chunk_piece(after, chunk[i].start, sizes[i])
            pairs.append(Plane(cp, me, after, piece, sizes[i], WIDE, 3 - step, sems[i // 2]))
        inner, rows = row_chunks(srow, 1, 1, sizes), row_chunks(rowp, 0, 0, sizes)
        last = row_chunks(grow, 7, 2, sizes)
        thirds = [Product(srow, panel, chunk[c].start, sizes[c]) for c in range(count)]
        inwards = [Product(rowp, hcol, chunk[c].start, sizes[c]) for c in range(count)]
        own_piece, own_block = after.at[mine], rowp.at[:, own_rows]
        blocks = [filters[step].astype(F32), others[step].astype(F32)]
        keep = [jnp.where(me.zl == 0, m[:, :4], m[:, 4:]) for m in blocks]
        left = jnp.where(me.zl == 0, keep[0], keep[1])
        right = jnp.where(me.zl == 0, keep[1], keep[0])
        early = first.total
        cut = chunk[-1].start
        upper, lower = Product(grow, after, 0, cut), Product(grow, after, cut, sizes[-1])

        def square_chunk(c):
            tail = Product(rowp, panel, chunk[c].start, sizes[c])
            tail.total = early[chunk[c]]
            tail.blocks(me, LATE)
            srow[chunk[c], own_rows] = tail.total.astype(BF)
            inner[c].start()
            square[chunk[c]] = tail.total

        def third_chunk(c):
            inner[c].arrive()
            thirds[c].tiles(me, 0, 0, 1, 3, 2)

        def dens_chunk(c):
            inner[c].shared()
            thirds[c].tiles(me, 1, 0, 1, 3, 2)
            lo = chunk[c].start
            while lo < chunk[c].stop:
                hi = min(lo // BS * BS + BS, chunk[c].stop)
                mask = jnp.concatenate([mask_row(left, lo // BS), mask_row(right, lo // BS)], axis=1)
                third = thirds[c].total[lo - chunk[c].start : hi - chunk[c].start]
                dens = (mask * (3.0 * square[lo:hi] - 2.0 * third)).astype(BF)
                own_piece[lo:hi] = dens
                own_block[lo:hi] = dens
                lo = hi

        def rows_start(c):
            if c == count - 1:
                drain_rows(srow, 1)
            rows[c].start()

        def inward_own(c):
            inwards[c].tiles(me, 0, 0, 1, 3, 2)

        def inward(c):
            inwards[c].tiles(me, 1, 0, 1, 3, 2)
            grow[chunk[c], own_rows] = inwards[c].total.astype(BF)
            last[c].start()

        def give(lo, hi):
            for owner in range(lo // OWN, hi // OWN):
                src = etile.at[owner * OWN : (owner + 1) * OWN]
                target = me.at(owner // 2, me.y, me.z, owner % 2)

                @pl.when(me.own != owner)
                def _():
                    cp.send(src, eall.at[:, own_rows], 8, energy_sem, target)

        def energy_upper():
            for dk in range(2):
                upper.tiles(me, dk, 0, 1, 3, 2)
            etile[:cut] = upper.total.astype(BF)
            give(0, cut)

        def energy_lower_own():
            lower.tiles(me, 0, 0, 1, 3, 2)

        def energy_lower():
            lower.tiles(me, 1, 0, 1, 3, 2)
            etile[cut:] = lower.total.astype(BF)
            give(cut, ROWS)

        tasks = dict(ham_tasks)
        for name, pair in zip("PQW", pairs):
            tasks.update(pair.tasks(name))
        steps = dict(S=square_chunk, T=third_chunk, D=dens_chunk, R=rows_start, Go=inward_own, G=inward)
        for c in range(count):
            tasks.update({name + str(c): functools.partial(f, c) for name, f in steps.items()})
            tasks.update({"Ra" + str(c): rows[c].arrive, "Rs" + str(c): rows[c].shared})
            tasks.update({"La" + str(c): last[c].arrive, "Ls" + str(c): last[c].shared})
        if step == 0:
            first = Product(rowp, after)
            tasks.update(E=functools.partial(first.blocks, me, EARLY))
        tasks.update(U=energy_upper, Vo=energy_lower_own, V=energy_lower)
        run(tasks, ORDER_B if step == 0 else ORDER_C)
        cp.sent(after.at[: 15 * ROWS], 3 - step)

    for ham in hams:
        ham.drain()
    drain_rows(rowp, 0)
    drain_rows(grow, 7)
    eall[:, own_rows] = etile[pl.ds(pl.multiple_of(me.own * OWN, OWN), OWN)]
    same = lax.broadcasted_iota(jnp.int32, (OWN, OWN), 0) == lax.broadcasted_iota(jnp.int32, (OWN, OWN), 1)
    loads[4].wait()
    loads[5].wait()
    atom_of = jnp.sum(jnp.where(same, atoms[...].astype(F32), 0.0), axis=1, keepdims=True)
    cp.sent(filters, 6)
    cp.arrive(eall.at[:, : 7 * WIDE], energy_sem)
    for b in range(8):
        for zl in range(2):
            energy_out[:, (zl * 8 + b) * SLIM : (zl * 8 + b + 1) * SLIM] = eall[
                :, b * WIDE + zl * SLIM : b * WIDE + (zl + 1) * SLIM
            ]
    wide = energy_out[...].astype(F32)
    lane = lax.broadcasted_iota(jnp.int32, (OWN, ATOM_DEV), 1).astype(F32)
    for axis in range(3):
        per_row = jnp.sum(deriv[axis].astype(F32) * wide, axis=1, keepdims=True)
        forces_out[axis : axis + 1] = jnp.sum(jnp.where(atom_of == lane, per_row, 0.0), axis=0, keepdims=True)
    cp.sent(eall.at[:, : 7 * WIDE], 8)


def body(hamil, guess, pattern, filters, deriv, atom_of_row):
    args = (hamil, guess, pattern.T, filters.transpose(0, 2, 1), deriv, atom_of_row.reshape(1, OWN))
    vmem = pl.BlockSpec(memory_space=pltpu.VMEM)
    sems = 3 * max(map(len, SIZES)) * ROW + (sum(map(len, SIZES)) // 2 + 2) * PLANE + 2
    return pl.pallas_call(
        kernel,
        out_shape=(
            jax.ShapeDtypeStruct((OWN, N), BF),
            jax.ShapeDtypeStruct((3, ATOM_DEV), F32),
        ),
        in_specs=[pl.BlockSpec(memory_space=pl.ANY)] * 6,
        out_specs=(vmem, vmem),
        scratch_shapes=[pltpu.VMEM(arg.shape, arg.dtype) for arg in args]
        + [
            pltpu.VMEM((ROWS, N), BF),
            pltpu.VMEM((2, N, WIDE), BF),
            pltpu.VMEM((ROWS, N), BF),
            pltpu.VMEM((ROWS, N), BF),
            pltpu.VMEM((N, WIDE), BF),
            pltpu.VMEM((ROWS, WIDE), F32),
            pltpu.VMEM((ROWS, WIDE), BF),
            pltpu.VMEM((OWN, N), BF),
            pltpu.VMEM(args[3].shape, args[3].dtype),
            pltpu.SemaphoreType.DMA((6,)),
            pltpu.SemaphoreType.DMA((9,)),
            pltpu.SemaphoreType.DMA((sems,)),
        ],
        compiler_params=pltpu.CompilerParams(
            collective_id=0, has_side_effects=True, vmem_limit_bytes=60 * 1024 * 1024
        ),
    )(*args)


def solution(mesh):
    return jax.shard_map(
        body,
        mesh=mesh,
        in_specs=(
            P("row", "col"),
            P("row", "col"),
            P("row", "col"),
            P(None, "row", "col"),
            P(None, ("row", "col"), None),
            P(("row", "col")),
        ),
        out_specs=(P(("row", "col"), None), P(None, ("row", "col"))),
        check_vma=False,
    )
```
